512 devices in a mesh: lat: 4 (over x), lon: 32 (over z, core), lev: 4 (over y).
Axes of the slice: x: 4, y: 4, z: 16, core: 2. Of those that a mesh axis runs over, the one named last changes fastest.
Arguments:
- fields: bfloat16 [24, 64, 40960], P('lev', 'lon', 'lat'), may hold values from -6 to 6
- slot_level: int32 [24], P('lev'), may hold values from -1 to 13, as said below
- embed_weight: bfloat16 [80, 512], replicated, may hold values from -0.625 to 0.625
- level_encoding: bfloat16 [14, 512], replicated, may hold values from -6 to 6
- latent_queries: bfloat16 [3, 512], replicated, may hold values from -400 to 400
- qkv_weight: bfloat16 [3, 512, 512], P(None, ('lon', 'lev')), may hold values from -0.25 to 0.25
- out_weight: bfloat16 [512, 512], P(('lon', 'lev')), may hold values from -0.25 to 0.25
Outputs:
- latents: bfloat16 [3, 512, 64, 512], P(None, ('lat', 'lon', 'lev'))
The draws below stay inside these ranges and needn't reach their ends.
Inputs may be any that keep to these rules, and one draw needn't show every extreme that they name: `slot_level`: each lev device's 6 slots hold its levels first and -1 after them; every device holds 1 to 6 levels, some device exactly 6; every level 0 to 13 is held by exactly one slot.
All inputs are finite; a program needn't handle non-finite values.
Results may differ from the reference program's by a relative error of at most 0.013.
The reference program's roundings to bfloat16 on the way count: a program that leaves them out, or rounds other values in their place, can miss the bound.
Values may be sent and summed in bfloat16 or wider, within the bound.
A program may use at most 64 MiB of HBM per device.

```python
import math
import jax
import jax.numpy as jnp
from jax import lax

D = 512
HEADS = 16
IN = 80
LATENT = 3
LEVELS = 14
SLOTS = 6
NLATP = 512
NLONP = 64
N_LEV = 4


def draw_slot_level(key, part):
    key = jax.random.fold_in(key, 7)
    key_pick, key_busy, key_perm = jax.random.split(key, 3)
    remaining = LEVELS - SLOTS
    listing = [[a, b, remaining - a - b] for a in range(1, SLOTS + 1) for b in range(1, SLOTS + 1) if 1 <= remaining - a - b <= SLOTS]
    compositions = jnp.array(listing, dtype=jnp.int32)
    pick = jax.random.randint(key_pick, (), 0, compositions.shape[0])
    others_count = compositions[pick]
    busiest = jax.random.randint(key_busy, (), 0, N_LEV)
    device_ids = jnp.arange(N_LEV, dtype=jnp.int32)
    padded = jnp.concatenate([others_count, jnp.zeros((1,), jnp.int32)])
    shifted = jnp.where(device_ids < busiest, padded[device_ids], padded[device_ids - 1])
    counts = jnp.where(device_ids == busiest, SLOTS, shifted).astype(jnp.int32)
    starts = jnp.cumsum(counts) - counts
    ordering = jax.random.permutation(key_perm, LEVELS).astype(jnp.int32)
    slot_ids = jnp.arange(SLOTS, dtype=jnp.int32)
    position = jnp.clip(starts[:, None] + slot_ids[None, :], 0, LEVELS - 1)
    held = ordering[position]
    table_out = jnp.where(slot_ids[None, :] < counts[:, None], held, -1)
    return table_out.reshape(N_LEV * SLOTS).astype(jnp.int32)


def draw_latent_queries(key, part):
    key = jax.random.fold_in(key, 13)
    key_base = jax.random.fold_in(key, 0)
    values = jnp.clip(jax.random.normal(key_base, (LATENT, D), jnp.float32), -6.0, 6.0)
    return values.astype(jnp.bfloat16)


def steps_of(key, dims, shards, smallest, high):
    def one(axis_at, blocks):
        steps = jax.random.uniform(jax.random.fold_in(jax.random.fold_in(key, 6), axis_at), (blocks,), jnp.float32, smallest / len(shards), high / len(shards))
        return jnp.repeat(jnp.exp(steps), dims[axis_at] // blocks).reshape((-1,) + (1,) * (len(dims) - axis_at - 1))

    gain = one(*shards[0])
    for cut in shards[1:]:
        gain = gain * one(*cut)
    return gain


def bell_draw(rng, dims, spread, bound, cuts=(), kind=jnp.bfloat16):
    loudness = steps_of(rng, dims, cuts, -0.22, 0.18) if cuts else 1.0
    values = jax.random.normal(rng, dims, jnp.float32) * spread * loudness
    return jnp.minimum(jnp.maximum(values, -bound), bound).astype(kind)


def setup_inputs(seed: int = 0) -> dict:
    streams_of = jax.random.split(jax.random.key(seed), 8)
    return {
        "fields": bell_draw(streams_of[0], (N_LEV * SLOTS, NLONP, NLATP * IN), 1.0, 6.0, ((0, 4), (1, 32), (2, 4))),
        "slot_level": draw_slot_level(jax.random.fold_in(streams_of[7], 71), 0),
        "embed_weight": bell_draw(streams_of[2], (IN, D), IN ** -0.5, 0.625),
        "level_encoding": bell_draw(streams_of[3], (LEVELS, D), 1.0, 6.0),
        "latent_queries": draw_latent_queries(jax.random.fold_in(streams_of[7], 71), 0),
        "qkv_weight": bell_draw(streams_of[5], (3, D, D), D ** -0.5, 0.25, ((1, 128),)),
        "out_weight": bell_draw(streams_of[6], (D, D), D ** -0.5, 0.25, ((0, 128),)),
    }


def reference(fields, slot_level, embed_weight, level_encoding, latent_queries, qkv_weight, out_weight):
    head_dim = D // HEADS
    level_ids = jnp.arange(LEVELS, dtype=jnp.int32)
    slot_ids = jnp.arange(N_LEV * SLOTS, dtype=jnp.int32)
    slot_of = lax.optimization_barrier(jnp.sum(jnp.where(slot_level[None, :] == level_ids[:, None], slot_ids[None, :], 0), axis=1)).astype(jnp.int32)
    picked = fields[slot_of]
    queries = jnp.dot(latent_queries, qkv_weight[0].T, preferred_element_type=jnp.float32).astype(jnp.bfloat16)
    query_heads = queries.astype(jnp.float32).reshape(LATENT, HEADS, head_dim)
    key_weight = qkv_weight[1]
    value_weight = qkv_weight[2]
    encoding = level_encoding.astype(jnp.float32)

    def column(block):
        patch_rows = block.reshape(LEVELS * NLATP, IN)
        embedded = jnp.dot(patch_rows, embed_weight, preferred_element_type=jnp.float32).reshape(LEVELS, NLATP, D)
        embedded = (embedded + encoding[:, None, :]).astype(jnp.bfloat16).reshape(LEVELS * NLATP, D)
        keys = jnp.dot(embedded, key_weight.T, preferred_element_type=jnp.float32).astype(jnp.bfloat16)
        values = jnp.dot(embedded, value_weight.T, preferred_element_type=jnp.float32).astype(jnp.bfloat16)
        keys = keys.astype(jnp.float32).reshape(LEVELS, NLATP, HEADS, head_dim)
        values = values.astype(jnp.float32).reshape(LEVELS, NLATP, HEADS, head_dim)
        scores = jnp.einsum('ahj,lrhj->ahlr', query_heads, keys, precision=lax.Precision.HIGHEST) / math.sqrt(head_dim)
        highest = lax.optimization_barrier(jnp.max(scores, axis=2, keepdims=True))
        expo = jnp.exp(scores - highest)
        summed = lax.optimization_barrier(jnp.sum(expo, axis=2))
        weighted = jnp.einsum('ahlr,lrhj->arhj', expo, values, precision=lax.Precision.HIGHEST)
        mixed = weighted / jnp.transpose(summed, (0, 2, 1))[..., None]
        mixed = mixed.astype(jnp.bfloat16).reshape(LATENT * NLATP, D)
        projected = jnp.dot(mixed, out_weight.T, preferred_element_type=jnp.float32).astype(jnp.bfloat16)
        return projected.reshape(LATENT, NLATP, D)
    columns = lax.map(column, jnp.transpose(picked, (1, 0, 2)))
    return jnp.transpose(columns, (1, 2, 0, 3))
```

```python
import functools
import math

import jax
import jax.numpy as jnp
from jax import lax
from jax.experimental import pallas as pl
from jax.experimental.pallas import tpu as pltpu
from jax.sharding import PartitionSpec as P

MESH = pl.DeviceIdType.MESH
F32 = jnp.float32
BF16 = jnp.bfloat16
NZ, NY, NX, NC = 16, 4, 4, 2
IN = 80
D = 512
LEVELS = 14
HEADS = 16
LATENT = 3
UNITS = 8 * IN
ROW = NZ * IN
ROWL = ROW + 128


def iota(shape, dim):
    return lax.broadcasted_iota(jnp.int32, shape, dim)


def nt(a, b):
    return lax.dot_general(a, b, (((1,), (1,)), ((), ())), preferred_element_type=F32)


def far_first(t):
    half = (t + 1) // 2
    return 8 + half * (1 - 2 * (t % 2))


def exchange_kernel(
    fields, slot_level, latent, qkv, out_w,
    w_all, q_all, f_all,
    tile, wy, regroup, f0, fy, fs,
    wz_s, wz_r, wy_s, wy_r, wx_s, wx_r, wc_s, wc_r, fy_s, fy_r, fz_s, fz_r,
):
    x = lax.axis_index("lat")
    lon = lax.axis_index("lon")
    y = lax.axis_index("lev")
    z = lon // 2
    c = lon % 2

    def device(dx=0, dy=0, dz=0, dc=0):
        return {
            "lat": (x + dx) % NX,
            "lon": ((z + dz) % NZ) * 2 + (c + dc) % 2,
            "lev": (y + dy) % NY,
        }

    barrier = pltpu.get_barrier_semaphore()

    def greet(dev):
        pl.semaphore_signal(barrier, inc=1, device_id=dev, device_id_type=MESH)

    def greet_z(t, carry):
        greet(device(dz=t))
        return carry

    def greet_yc(t, carry):
        greet(device(dy=t // 2, dc=t % 2))
        return carry

    def greet_x(t, carry):
        greet(device(dx=t))
        return carry

    lax.fori_loop(1, NZ, greet_z, 0)
    lax.fori_loop(1, 8, greet_yc, 0)
    lax.fori_loop(1, NX, greet_x, 0)

    wq = qkv[0].astype(F32)
    lat = latent[...].astype(F32)
    lane = iota((4, 128), 1)
    q = jnp.zeros((4, 128), F32)
    for a in range(LATENT):
        col = jnp.sum(wq * lat[a : a + 1, :], axis=1, keepdims=True)
        q = jnp.where(lane == a, col, q)
    for part in range(NX):
        cut = slice(part * 128, part * 128 + 128)
        tile[part] = jnp.concatenate(
            [q, qkv[1, :, cut].astype(F32), qkv[2, :, cut].astype(F32), out_w[:, cut].astype(F32)], axis=0
        ).astype(BF16)

    for g in range(2):
        blocks = []
        for e in range(8):
            at = (8 * g + e) * UNITS
            rows = [fields[s, :, at : at + UNITS].astype(F32) for s in range(6)]
            blocks.append(jnp.concatenate(rows + [jnp.zeros((4, UNITS), F32)], axis=0))
        for d in range(8):
            f0[d, :, g * UNITS : (g + 1) * UNITS] = jnp.concatenate(
                [blocks[e][:, d * IN : (d + 1) * IN] for e in range(8)], axis=1
            ).astype(BF16)
    slot_of_row = iota((16, 128), 0) // 2
    levels = jnp.full((16, 128), -1.0, F32)
    for s in range(6):
        levels = jnp.where(slot_of_row == s, slot_level[s].astype(F32), levels)
    for d in range(8):
        f0[d, :, ROW:ROWL] = levels.astype(BF16)

    pl.semaphore_wait(barrier, NZ - 1 + 7 + NX - 1)

    def wz_copy(s):
        return pltpu.make_async_remote_copy(
            src_ref=tile.at[x], dst_ref=wy.at[y, z], send_sem=wz_s.at[s], recv_sem=wz_r.at[s],
            device_id=device(dz=s), device_id_type=MESH,
        )

    def fy_copy(t):
        dev = device(dy=t // 2, dc=t % 2)
        d = (dev["lon"] % 2) * 4 + dev["lev"]
        return pltpu.make_async_remote_copy(
            src_ref=f0.at[d], dst_ref=fy.at[c * 4 + y], send_sem=fy_s.at[t], recv_sem=fy_r.at[t],
            device_id=dev, device_id_type=MESH,
        )

    def wy_copy(t):
        return pltpu.make_async_remote_copy(
            src_ref=wy.at[y], dst_ref=wy.at[y], send_sem=wy_s.at[t], recv_sem=wy_r.at[t],
            device_id=device(dy=t), device_id_type=MESH,
        )

    def fz_copy(s):
        return pltpu.make_async_remote_copy(
            src_ref=fs.at[(z + s) % NZ], dst_ref=f_all.at[z], send_sem=fz_s.at[s], recv_sem=fz_r.at[s],
            device_id=device(dz=s), device_id_type=MESH,
        )

    def lanes(part):
        return pl.ds(pl.multiple_of(part * 128, 128), 128)

    def wx_copy(t):
        return pltpu.make_async_remote_copy(
            src_ref=regroup.at[pl.ds(1, 3)], dst_ref=w_all.at[:, :, c, :, lanes(x)],
            send_sem=wx_s.at[t], recv_sem=wx_r.at[t], device_id=device(dx=t), device_id_type=MESH,
        )

    def wc_copy(t):
        part = (x + NX - t) % NX
        return pltpu.make_async_remote_copy(
            src_ref=w_all.at[:, :, c, :, lanes(part)], dst_ref=w_all.at[:, :, c, :, lanes(part)],
            send_sem=wc_s.at[t], recv_sem=wc_r.at[t], device_id=device(dc=1), device_id_type=MESH,
        )

    def wc_land(t):
        part = (x + NX - t) % NX
        return pltpu.make_async_remote_copy(
            src_ref=w_all.at[:, :, 1 - c, :, lanes(part)], dst_ref=w_all.at[:, :, 1 - c, :, lanes(part)],
            send_sem=wc_s.at[t], recv_sem=wc_r.at[t], device_id=device(dc=1), device_id_type=MESH,
        )

    def qc_copy():
        return pltpu.make_async_remote_copy(
            src_ref=q_all.at[:, c], dst_ref=q_all.at[:, c],
            send_sem=wc_s.at[NX], recv_sem=wc_r.at[NX], device_id=device(dc=1), device_id_type=MESH,
        )

    def loop(lo, hi, act):
        def body(t, carry):
            act(t)
            return carry

        lax.fori_loop(lo, hi, body, 0)

    loop(0, NZ - 1, lambda t: wz_copy(far_first(t)).start())
    loop(1, 8, lambda t: fy_copy(t).start())
    wy[y, z] = tile[x]
    fy[c * 4 + y] = f0[c * 4 + y]

    loop(1, NZ, lambda s: wz_copy(s).wait_recv())
    loop(1, NY, lambda t: wy_copy(t).start())

    loop(1, 8, lambda t: fy_copy(t).wait_recv())
    slots = fy[:, :, ROW:ROWL].astype(F32).reshape(128, 128)
    at_row = iota((128, 128), 0)
    at_lane = iota((128, 128), 1)
    pick = (
        (slots == (at_lane % 16).astype(F32))
        & (at_row // 64 == at_lane // 32)
        & (at_row % 2 == (at_lane // 16) % 2)
    )
    pick = jnp.transpose(jnp.where(pick, 1.0, 0.0))[:64].astype(BF16)
    kept = jnp.dot(pick, fy[:, :, 0:ROW].reshape(128, ROW), preferred_element_type=F32)
    blank = jnp.zeros((16, 64), F32)
    for to in range(NZ):
        fs[to] = jnp.concatenate(
            [kept[16 * u : 16 * u + 16, to * IN : (to + 1) * IN] for u in range(4)] + [blank], axis=1
        ).astype(BF16)
    loop(0, NZ - 1, lambda t: fz_copy(far_first(t)).start())
    f_all[z] = fs[z]

    loop(1, NY, lambda t: wy_copy(t).wait_recv())

    def regroup_one(i, carry):
        rows = [wy[k, i].astype(F32) for k in range(NY)]
        for m in range(4):
            regroup[m, i] = jnp.concatenate([r[4 * m : 4 * m + 4] for r in rows], axis=0).astype(BF16)
        return carry

    lax.fori_loop(0, NZ, regroup_one, 0)
    loop(1, NX, lambda t: wx_copy(t).start())
    w_all[:, :, c, :, lanes(x)] = regroup[1:4]
    q_all[:, c] = regroup[0]
    wc_copy(0).start()
    qc_copy().start()

    def forward(t):
        wx_copy(t).wait_recv()
        wc_copy(t).start()

    loop(1, NX, forward)
    loop(1, NZ, lambda s: fz_copy(s).wait_recv())
    loop(0, NX, lambda t: wc_land(t).wait_recv())
    qc_copy().wait_recv()

    loop(1, NZ, lambda s: wz_copy(s).wait_send())
    loop(1, NZ, lambda s: fz_copy(s).wait_send())
    loop(1, 8, lambda t: fy_copy(t).wait_send())
    loop(1, NY, lambda t: wy_copy(t).wait_send())
    loop(1, NX, lambda t: wx_copy(t).wait_send())
    loop(0, NX, lambda t: wc_copy(t).wait_send())
    qc_copy().wait_send()


def exchange(fields, slot_level, latent, qkv, out_w):
    dma = pltpu.SemaphoreType.DMA
    vmem = pl.BlockSpec(memory_space=pltpu.VMEM)
    return pl.pallas_call(
        exchange_kernel,
        out_shape=(
            jax.ShapeDtypeStruct((3, NZ, NC, 16, D), BF16),
            jax.ShapeDtypeStruct((NZ, NC, 16, 128), BF16),
            jax.ShapeDtypeStruct((NZ, 16, 384), BF16),
        ),
        in_specs=[vmem, pl.BlockSpec(memory_space=pltpu.SMEM), vmem, vmem, vmem],
        out_specs=(vmem, vmem, vmem),
        scratch_shapes=[
            pltpu.VMEM((NX, 16, 128), BF16),
            pltpu.VMEM((NY, NZ, 16, 128), BF16),
            pltpu.VMEM((4, NZ, 16, 128), BF16),
            pltpu.VMEM((8, 16, ROWL), BF16),
            pltpu.VMEM((8, 16, ROWL), BF16),
            pltpu.VMEM((NZ, 16, 384), BF16),
            dma((NZ,)), dma((NZ,)),
            dma((NY,)), dma((NY,)),
            dma((NX,)), dma((NX,)),
            dma((NX + 1,)), dma((NX + 1,)),
            dma((8,)), dma((8,)),
            dma((NZ,)), dma((NZ,)),
        ],
        compiler_params=pltpu.CompilerParams(
            collective_id=0, has_side_effects=True, vmem_limit_bytes=32 * 1024 * 1024
        ),
        name="exchange",
    )(fields, slot_level, latent, qkv, out_w)


def compute_kernel(w, qt, f, embed_weight, level_encoding, out, shifted):
    scale = 1.0 / math.sqrt(D // HEADS)
    r = iota((LEVELS * 16, 256), 0)
    j = iota((LEVELS * 16, 256), 1)
    perm = jnp.where(j == (r % 16) * 16 + r // 16, 1.0, 0.0).astype(BF16)
    rows = jnp.dot(perm, f[...], preferred_element_type=F32).astype(BF16)
    shifted[...] = jnp.zeros_like(shifted)
    starts = (0, IN, 2 * IN - 128, 3 * IN - 128)
    for u in range(4):
        shifted[u, starts[u] : starts[u] + IN, :] = embed_weight[...]
    windows = ((0, 128), (0, 256), (128, 256), (128, 384))
    encoding = jnp.broadcast_to(
        level_encoding[...].astype(F32)[:, None, :], (LEVELS, 16, D)
    ).reshape(LEVELS * 16, D)

    fi = iota((D, 128), 0)
    li = iota((D, 128), 1)
    qv = qt[...].astype(F32)
    qblk = jnp.zeros((D, 128), F32)
    for a in range(LATENT):
        qblk = jnp.where(li == a * HEADS + fi // 32, qv[:, a : a + 1], qblk)
    qblk = qblk.astype(BF16)
    ki = iota((256, D), 0) % 128
    head = iota((256, D), 1) // 32
    spread = [jnp.where(ki == a * HEADS + head, 1.0, 0.0).astype(BF16) for a in range(LATENT)]

    mixed = [[] for _ in range(LATENT)]
    for u in range(4):
        lo, hi = windows[u]
        emb = (
            jnp.dot(rows[:, lo:hi], shifted[u, : hi - lo, :], preferred_element_type=F32) + encoding
        ).astype(BF16)
        keys = nt(emb, w[0]).astype(BF16)
        scores = (jnp.dot(keys, qblk, preferred_element_type=F32) * scale).reshape(LEVELS, 16, 128)
        highest = jnp.max(scores, axis=0, keepdims=True)
        expo = jnp.exp(scores - highest)
        weight = (expo / jnp.sum(expo, axis=0, keepdims=True)).reshape(LEVELS * 16, 128)
        top = weight.astype(BF16)
        low = (weight - top.astype(F32)).astype(BF16)
        both = jnp.concatenate([top, low], axis=1)
        values = nt(emb, w[1]).astype(BF16).astype(F32)
        for a in range(LATENT):
            wide = jnp.dot(both, spread[a], preferred_element_type=F32)
            mixed[a].append(jnp.sum((wide * values).reshape(LEVELS, 16, D), axis=0).astype(BF16))
    r = iota((64, 64), 0)
    j = iota((64, 64), 1)
    order = jnp.where(j == (r % 4) * 16 + r // 4, 1.0, 0.0).astype(BF16)
    for a in range(LATENT):
        block = jnp.dot(order, jnp.concatenate(mixed[a], axis=0), preferred_element_type=F32).astype(BF16)
        out[a] = nt(block, w[2]).astype(BF16)


def compute(w, qt, f, embed_weight, level_encoding):
    vmem = pl.BlockSpec(memory_space=pltpu.VMEM)
    return pl.pallas_call(
        compute_kernel,
        out_shape=jax.ShapeDtypeStruct((LATENT, 64, D), BF16),
        in_specs=[vmem] * 5,
        out_specs=vmem,
        scratch_shapes=[pltpu.VMEM((4, 256, D), BF16)],
        compiler_params=pltpu.CompilerParams(vmem_limit_bytes=32 * 1024 * 1024),
        cost_estimate=pl.CostEstimate(flops=2 * 10**9, bytes_accessed=3 * 10**6, transcendentals=10**5),
        name="attend",
    )(w, qt, f, embed_weight, level_encoding)


def on_device(fields, slot_level, embed_weight, level_encoding, latent_queries, qkv_weight, out_weight):
    w, q, f = exchange(fields, slot_level, latent_queries, qkv_weight, out_weight)
    out = compute(
        w.reshape(3, D, D), q.reshape(D, 128), f.reshape(NZ * 16, 384), embed_weight, level_encoding
    )
    return out.reshape(LATENT, 1, 64, D)


def solution(mesh):
    in_specs = (
        P("lev", "lon", "lat"),
        P("lev"),
        P(),
        P(),
        P(),
        P(None, ("lon", "lev"), None),
        P(("lon", "lev"), None),
    )
    out_specs = P(None, ("lat", "lon", "lev"), None, None)
    return jax.shard_map(
        on_device, mesh=mesh, in_specs=in_specs, out_specs=out_specs, check_vma=False
    )
```

```python
import math

import jax
import jax.numpy as jnp
from jax import lax
from jax.experimental import pallas as pl
from jax.experimental.pallas import tpu as pltpu
from jax.sharding import PartitionSpec as P

MESH = pl.DeviceIdType.MESH
F32 = jnp.float32
BF16 = jnp.bfloat16
NZ, NY, NX, NC = 16, 4, 4, 2
NXY = NX * NY
IN = 80
D = 512
LEVELS = 14
HEADS = 16
LATENT = 3
UNITS = 8 * IN
ROWS = LEVELS * 16
VMEM_LIMIT = 60 * 1024 * 1024


def iota(shape, dim):
    return lax.broadcasted_iota(jnp.int32, shape, dim)


def one_hot(mask):
    return jnp.where(mask, 1.0, 0.0).astype(BF16)


def dot(a, b):
    return jnp.dot(a, b, preferred_element_type=F32)


def nt(a, b):
    return lax.dot_general(a, b, (((1,), (1,)), ((), ())), preferred_element_type=F32)


def offset(k):
    return (NZ + (k % 2) * ((k + 1) // 2) - (1 - k % 2) * (k // 2)) % NZ


def loop(lo, hi, act):
    def body(t, carry):
        act(t)
        return carry

    lax.fori_loop(lo, hi, body, 0)


def kernel(
    fields_h, slot_h, latent_h, qkv_h, out_w_h, embed_h, encode_h,
    out,
    fields, slot_level, latent, qkv, out_w, embed, encode,
    tile, wz, pack, w_all, q_all, f0a, f0b, fya, fyb, kept, fs, fz,
    shifted, emb, qblk, spread, natural, mixed,
    in_s, wz_s, wz_r, wp_s, wp_r, wq_s, wq_r, wc_s, wc_r, fy_s, fy_r, fz_s, fz_r,
):
    x = lax.axis_index("lat")
    lon = lax.axis_index("lon")
    y = lax.axis_index("lev")
    z = lon // 2
    c = lon % 2

    def device(dx=0, dy=0, dz=0, dc=0):
        return {
            "lat": (x + dx) % NX,
            "lon": ((z + dz) % NZ) * 2 + (c + dc) % 2,
            "lev": (y + dy) % NY,
        }

    barrier = pltpu.get_barrier_semaphore()

    def greet(dev):
        pl.semaphore_signal(barrier, inc=1, device_id=dev, device_id_type=MESH)

    loop(1, NZ, lambda k: greet(device(dz=offset(NZ - k))))
    loop(1, NXY, lambda t: greet(device(dx=t // NY, dy=t % NY)))
    loop(0, NY, lambda t: greet(device(dy=t, dc=1)))

    loads = [
        pltpu.make_async_copy(src, dst, in_s.at[i])
        for i, (src, dst) in enumerate(
            (
                (qkv_h, qkv), (out_w_h, out_w), (latent_h, latent), (slot_h, slot_level),
                (fields_h, fields), (embed_h, embed), (encode_h, encode),
            )
        )
    ]
    for load in loads:
        load.start()
    for load in loads[:3]:
        load.wait()

    wq = qkv[0].astype(F32)
    lat = latent[...].astype(F32)
    lane = iota((4, 128), 1)
    q = jnp.zeros((4, 128), F32)
    for a in range(LATENT):
        col = jnp.sum(wq * lat[a : a + 1, :], axis=1, keepdims=True)
        q = jnp.where(lane == a, col, q)
    for part in range(NX):
        cut_at = slice(part * 128, part * 128 + 128)
        tile[part] = jnp.concatenate(
            [q, qkv[1, :, cut_at].astype(F32), qkv[2, :, cut_at].astype(F32), out_w[:, cut_at].astype(F32)],
            axis=0,
        ).astype(BF16)
    wz[0] = tile[x]

    for load in loads[3:5]:
        load.wait()
    for half, f0 in ((1, f0a), (0, f0b)):
        blocks = []
        for e in range(8):
            to = (z + NZ - offset(8 * half + e)) % NZ
            at = pl.ds(pl.multiple_of(to * UNITS, 128), UNITS)
            rows = [fields[s, :, at].astype(F32) for s in range(6)]
            blocks.append(jnp.concatenate(rows + [jnp.zeros((4, UNITS), F32)], axis=0))
        for d in range(8):
            f0[d, :, 0:UNITS] = jnp.concatenate(
                [blocks[e][:, d * IN : (d + 1) * IN] for e in range(8)], axis=1
            ).astype(BF16)
    slot_of_row = iota((16, 128), 0) // 2
    levels = jnp.full((16, 128), -1.0, F32)
    for s in range(6):
        levels = jnp.where(slot_of_row == s, slot_level[s].astype(F32), levels)
    for d in range(8):
        f0a[d, :, UNITS:] = levels.astype(BF16)
    fya[c * 4 + y] = f0a[c * 4 + y]
    fyb[c * 4 + y] = f0b[c * 4 + y]

    def remote(src, dst, send, recv, dev):
        return pltpu.make_async_remote_copy(
            src_ref=src, dst_ref=dst, send_sem=send, recv_sem=recv, device_id=dev, device_id_type=MESH
        )

    def wz_copy(k):
        return remote(tile.at[x], wz.at[k], wz_s.at[k], wz_r.at[k], device(dz=NZ - offset(k)))

    def fy_copy(t, half):
        dev = device(dy=t // 2, dc=t % 2)
        d = (dev["lon"] % 2) * 4 + dev["lev"]
        f0, fy = ((f0b, fyb), (f0a, fya))[half]
        return remote(f0.at[d], fy.at[c * 4 + y], fy_s.at[half, t], fy_r.at[half, t], dev)

    def fz_copy(k):
        return remote(fs.at[k], fz.at[z], fz_s.at[k], fz_r.at[k], device(dz=NZ - offset(k)))

    lanes = pl.ds(pl.multiple_of(x * 128, 128), 128)

    def wp_copy(t, i):
        what, which = ((slice(0, 2), slice(0, 2)), (slice(0, 2), slice(2, 4)), (slice(2, 3), slice(0, 4)))[i]
        return remote(
            pack.at[what, which], w_all.at[what, c, y, which, :, lanes], wp_s.at[i, t], wp_r.at[i, t],
            device(dx=t // NY, dy=t % NY),
        )

    def wq_copy(t):
        return remote(pack.at[3], q_all.at[c, y], wq_s.at[t], wq_r.at[t], device(dy=t))

    def wc_copy(m, side):
        ref = q_all.at[side] if m == 3 else w_all.at[m, side]
        return remote(ref, ref, wc_s.at[m], wc_r.at[m], device(dc=1))

    def regroup(i):
        rows = [wz[4 * i + j].astype(F32) for j in range(4)]
        for m, at in ((3, 0), (0, 4), (1, 8), (2, 12)):
            block = jnp.concatenate([r[at : at + 4] for r in rows], axis=0).astype(BF16)
            pack[m, i] = block
            if m == 3:
                q_all[c, y, i] = block
            else:
                w_all[m, c, y, i, :, lanes] = block

    pl.semaphore_wait(barrier, NZ - 1 + NXY - 1 + NY)
    loop(1, NZ, lambda k: wz_copy(NZ - k).start())
    loop(1, 8, lambda t: fy_copy(t, 1).start())
    loop(1, 8, lambda t: fy_copy(t, 0).start())
    for load in loads[5:]:
        load.wait()
    shifted[...] = jnp.zeros_like(shifted)
    starts = (0, IN, 2 * IN - 128, 3 * IN - 128)
    for u in range(4):
        shifted[u, starts[u] : starts[u] + IN, :] = embed[...]

    def head_of(g):
        k = (g // 4) % NZ
        return (z + jnp.where(k % 2 == 1, (k + 1) // 2, NZ - k // 2)) % NZ

    g = iota((D, D), 0)
    natural[...] = one_hot(iota((D, D), 1) == head_of(g) * 32 + (g // 256) * 16 + (g // 64) % 4 * 4 + g % 4)
    ki = iota((256, D), 0) % 128
    head = head_of(iota((256, D), 1))
    for a in range(LATENT):
        spread[a] = one_hot(ki == a * HEADS + head)

    loop(1, 8, lambda t: fy_copy(t, 1).wait_recv())
    slots = fya[:, :, UNITS:].astype(F32).reshape(128, 128)
    at_row = iota((128, 128), 0)
    at_lane = iota((128, 128), 1)
    pick = (
        (slots == (at_lane % 16).astype(F32))
        & (at_row // 64 == at_lane // 32)
        & (at_row % 2 == (at_lane // 16) % 2)
    )
    pick = jnp.transpose(jnp.where(pick, 1.0, 0.0))[:64].astype(BF16)
    blank = jnp.zeros((16, 64), F32)

    def keep(half, fy):
        kept[...] = dot(pick, fy[:, :, 0:UNITS].reshape(128, UNITS))
        for e in range(8):
            fs[8 * half + e] = jnp.concatenate(
                [kept[16 * u : 16 * u + 16, e * IN : (e + 1) * IN] for u in range(4)] + [blank], axis=1
            ).astype(BF16)

    keep(1, fya)
    loop(0, 8, lambda k: fz_copy(NZ - 1 - k).start())
    loop(1, 8, lambda t: fy_copy(t, 0).wait_recv())
    keep(0, fyb)
    loop(1, 8, lambda k: fz_copy(8 - k).start())
    fz[z] = fs[0]

    loop(1, 8, lambda k: wz_copy(k).wait_recv())
    regroup(0)
    regroup(1)
    loop(1, NXY, lambda t: wp_copy(t, 0).start())
    loop(8, NZ, lambda k: wz_copy(k).wait_recv())
    regroup(2)
    regroup(3)
    loop(1, NXY, lambda t: wp_copy(t, 1).start())
    loop(1, NY, lambda t: wq_copy(t).start())
    loop(1, NXY, lambda t: wp_copy(t, 2).start())

    loop(1, NZ, lambda k: fz_copy(k).wait_recv())
    r = iota((ROWS, 256), 0)
    j = iota((ROWS, 256), 1)
    rows = dot(one_hot(j == (r % 16) * 16 + r // 16), fz[...].reshape(256, 384)).astype(BF16)
    encoding = jnp.broadcast_to(encode[...].astype(F32)[:, None, :], (LEVELS, 16, D)).reshape(ROWS, D)
    for u, (lo, hi) in enumerate(((0, 128), (0, 256), (128, 256), (128, 384))):
        emb[u] = (dot(rows[:, lo:hi], shifted[u, : hi - lo, :]) + encoding).astype(BF16)

    loop(1, NY, lambda t: wq_copy(t).wait_recv())
    wc_copy(3, c).start()
    loop(1, NXY, lambda t: wp_copy(t, 0).wait_recv())
    loop(1, NXY, lambda t: wp_copy(t, 1).wait_recv())
    wc_copy(0, c).start()
    wc_copy(1, c).start()
    wc_copy(3, 1 - c).wait_recv()
    wc_copy(0, 1 - c).wait_recv()
    wc_copy(1, 1 - c).wait_recv()

    scale = 1.0 / math.sqrt(D // HEADS)
    g = iota((D, 128), 0)
    at_lane = iota((D, 128), 1)
    qv = q_all[...].astype(F32).reshape(D, 128)
    found = jnp.zeros((D, 128), F32)
    for a in range(LATENT):
        found = jnp.where(at_lane == a * HEADS + head_of(g), qv[:, a : a + 1], found)
    qblk[...] = found.astype(BF16)
    k_w = w_all.at[0]
    v_w = w_all.at[1]
    for u in range(4):
        keys = nt(emb[u], k_w[...].reshape(D, D)).astype(BF16)
        scores = (dot(keys, qblk[...]) * scale).reshape(LEVELS, 16, 128)
        highest = jnp.max(scores, axis=0, keepdims=True)
        expo = jnp.exp(scores - highest)
        weight = (expo / jnp.sum(expo, axis=0, keepdims=True)).reshape(ROWS, 128)
        top = weight.astype(BF16)
        low = (weight - top.astype(F32)).astype(BF16)
        both = jnp.concatenate([top, low], axis=1)
        values = nt(emb[u], v_w[...].reshape(D, D)).astype(BF16).astype(F32)
        for a in range(LATENT):
            wide = dot(both, spread[a])
            mixed[a, 16 * u : 16 * u + 16] = jnp.sum(
                (wide * values).reshape(LEVELS, 16, D), axis=0
            ).astype(BF16)
    loop(1, NXY, lambda t: wp_copy(t, 2).wait_recv())
    wc_copy(2, c).start()
    r = iota((64, 64), 0)
    j = iota((64, 64), 1)
    order = one_hot(j == (r % 4) * 16 + r // 4)
    block = jnp.concatenate([dot(order, mixed[a]).astype(BF16) for a in range(LATENT)], axis=0)
    block = dot(block, natural[...]).astype(BF16)
    wc_copy(2, 1 - c).wait_recv()
    block = nt(block, w_all[2].reshape(D, D)).astype(BF16)
    out[...] = dot(block, natural[...]).astype(BF16).reshape(LATENT, 64, D)

    loop(1, NZ, lambda k: wz_copy(k).wait_send())
    loop(1, NZ, lambda k: fz_copy(k).wait_send())
    for half in range(2):
        loop(1, 8, lambda t: fy_copy(t, half).wait_send())
    for i in range(3):
        loop(1, NXY, lambda t: wp_copy(t, i).wait_send())
    loop(1, NY, lambda t: wq_copy(t).wait_send())
    for m in range(4):
        wc_copy(m, c).wait_send()


def encode_patches(*operands):
    dma = pltpu.SemaphoreType.DMA
    vmem = pltpu.VMEM
    fields, slot_level, latent, qkv, out_w, embed, encode = operands
    return pl.pallas_call(
        kernel,
        out_shape=jax.ShapeDtypeStruct((LATENT, 64, D), BF16),
        in_specs=[pl.BlockSpec(memory_space=pltpu.HBM)] * 7,
        out_specs=pl.BlockSpec(memory_space=pltpu.VMEM),
        scratch_shapes=[
            vmem(fields.shape, BF16),
            pltpu.SMEM(slot_level.shape, jnp.int32),
            vmem(latent.shape, BF16),
            vmem(qkv.shape, BF16),
            vmem(out_w.shape, BF16),
            vmem(embed.shape, BF16),
            vmem(encode.shape, BF16),
            vmem((NX, 16, 128), BF16),
            vmem((NZ, 16, 128), BF16),
            vmem((4, 4, 16, 128), BF16),
            vmem((3, NC, NY, 4, 16, D), BF16),
            vmem((NC, NY, 4, 16, 128), BF16),
            vmem((8, 16, UNITS + 128), BF16),
            vmem((8, 16, UNITS), BF16),
            vmem((8, 16, UNITS + 128), BF16),
            vmem((8, 16, UNITS), BF16),
            vmem((64, UNITS), F32),
            vmem((NZ, 16, 384), BF16),
            vmem((NZ, 16, 384), BF16),
            vmem((4, 256, D), BF16),
            vmem((4, ROWS, D), BF16),
            vmem((D, 128), BF16),
            vmem((LATENT, 256, D), BF16),
            vmem((D, D), BF16),
            vmem((LATENT, 64, D), BF16),
            dma((7,)),
            dma((NZ,)), dma((NZ,)),
            dma((3, NXY)), dma((3, NXY)),
            dma((NY,)), dma((NY,)),
            dma((4,)), dma((4,)),
            dma((2, 8)), dma((2, 8)),
            dma((NZ,)), dma((NZ,)),
        ],
        compiler_params=pltpu.CompilerParams(
            collective_id=0, has_side_effects=True, vmem_limit_bytes=VMEM_LIMIT
        ),
        cost_estimate=pl.CostEstimate(flops=3 * 10**9, bytes_accessed=10**6, transcendentals=10**5),
        name="encode_patches",
    )(*operands)


def on_device(fields, slot_level, embed_weight, level_encoding, latent_queries, qkv_weight, out_weight):
    out = encode_patches(
        fields, slot_level, latent_queries, qkv_weight, out_weight, embed_weight, level_encoding
    )
    return out.reshape(LATENT, 1, 64, D)


def solution(mesh):
    in_specs = (
        P("lev", "lon", "lat"),
        P("lev"),
        P(),
        P(),
        P(),
        P(None, ("lon", "lev"), None),
        P(("lon", "lev"), None),
    )
    out_specs = P(None, ("lat", "lon", "lev"), None, None)
    return jax.shard_map(
        on_device, mesh=mesh, in_specs=in_specs, out_specs=out_specs, check_vma=False
    )
```

```python
import math

import jax
import jax.numpy as jnp
from jax import lax
from jax.experimental import pallas as pl
from jax.experimental.pallas import tpu as pltpu
from jax.sharding import PartitionSpec as P

MESH = pl.DeviceIdType.MESH
F32 = jnp.float32
BF16 = jnp.bfloat16
NZ, NY, NX, NC = 16, 4, 4, 2
IN = 80
D = 512
LEVELS = 14
HEADS = 16
LATENT = 3
UNITS = 8 * IN
ROWS = LEVELS * 16
VMEM_LIMIT = 40 * 1024 * 1024


def iota(shape, dim):
    return lax.broadcasted_iota(jnp.int32, shape, dim)


def one_hot(mask):
    return jnp.where(mask, 1.0, 0.0).astype(BF16)


def dot(a, b):
    return jnp.dot(a, b, preferred_element_type=F32)


def nt(a, b):
    return lax.dot_general(a, b, (((1,), (1,)), ((), ())), preferred_element_type=F32)


def offset(k):
    return (NZ + (k % 2) * ((k + 1) // 2) - (1 - k % 2) * (k // 2)) % NZ


def loop(lo, hi, act):
    def body(t, carry):
        act(t)
        return carry

    lax.fori_loop(lo, hi, body, 0)


def kernel(
    fields_h, slot_h, latent_h, qkv_h, out_w_h, embed_h, encode_h,
    out,
    fields, slot_level, latent, qkv, out_w, embed, encode,
    tile, wz, pack, w_kv, w_o, q_all, f0, fy, whole, kept, fs, fz,
    shifted, emb, spread, natural_t, mixed,
    in_s, wz_s, wz_r, wp_s, wp_r, wy_s, wy_r, wx_s, wx_r, wc_s, wc_r, fy_s, fy_r, fz_s, fz_r,
):
    x = lax.axis_index("lat")
    lon = lax.axis_index("lon")
    y = lax.axis_index("lev")
    z = lon // 2
    c = lon % 2

    def device(dx=0, dy=0, dz=0, dc=0):
        return {
            "lat": (x + dx) % NX,
            "lon": ((z + dz) % NZ) * 2 + (c + dc) % 2,
            "lev": (y + dy) % NY,
        }

    barrier = pltpu.get_barrier_semaphore()

    def greet(dev):
        pl.semaphore_signal(barrier, inc=1, device_id=dev, device_id_type=MESH)

    loop(1, NZ, lambda k: greet(device(dz=offset(NZ - k))))
    loop(1, NX, lambda t: greet(device(dx=t)))
    loop(1, 8, lambda t: greet(device(dy=t // 2, dc=t % 2)))

    loads = [
        pltpu.make_async_copy(src, dst, in_s.at[i])
        for i, (src, dst) in enumerate(
            (
                (qkv_h, qkv), (out_w_h, out_w), (latent_h, latent), (slot_h, slot_level),
                (fields_h, fields), (embed_h, embed), (encode_h, encode),
            )
        )
    ]
    for load in loads:
        load.start()
    for load in loads[:3]:
        load.wait()

    wq = qkv[0].astype(F32)
    lat = latent[...].astype(F32)
    lane = iota((4, 128), 1)
    q = jnp.zeros((4, 128), F32)
    for a in range(LATENT):
        col = jnp.sum(wq * lat[a : a + 1, :], axis=1, keepdims=True)
        q = jnp.where(lane == a, col, q)
    for part in range(NX):
        cut_at = slice(part * 128, part * 128 + 128)
        tile[part] = jnp.concatenate(
            [q, qkv[1, :, cut_at].astype(F32), qkv[2, :, cut_at].astype(F32), out_w[:, cut_at].astype(F32)],
            axis=0,
        ).astype(BF16)
    wz[0] = tile[x]

    for load in loads[3:5]:
        load.wait()
    at_row = iota((4, 128), 0)
    slot_of_lane = iota((4, 128), 1) // 2
    levels = jnp.full((4, 128), -1.0, F32)
    for s in range(6):
        levels = jnp.where(slot_of_lane == s, slot_level[s].astype(F32), levels)
    for half in (1, 0):
        blocks = []
        for e in range(8):
            to = (z + NZ - offset(8 * half + e)) % NZ
            at = pl.ds(pl.multiple_of(to * UNITS, 128), UNITS)
            blocks.append(jnp.concatenate([fields[s, :, at].astype(F32) for s in range(6)], axis=0))
        for d in range(8):
            units = jnp.concatenate([blocks[e][:, d * IN : (d + 1) * IN] for e in range(8)], axis=1)
            last = units[:, 512:]
            spare = jnp.concatenate([last[0:4], last[4:8], last[8:12], levels], axis=1)
            f0[half, d] = jnp.concatenate([units[:, :512], spare], axis=0).astype(BF16)
    for half in range(2):
        fy[half, c * 4 + y] = f0[half, c * 4 + y]

    def remote(src, dst, send, recv, dev):
        return pltpu.make_async_remote_copy(
            src_ref=src, dst_ref=dst, send_sem=send, recv_sem=recv, device_id=dev, device_id_type=MESH
        )

    def wz_copy(k):
        return remote(tile.at[x], wz.at[k], wz_s.at[k], wz_r.at[k], device(dz=NZ - offset(k)))

    def fy_copy(t, half):
        dev = device(dy=t // 2, dc=t % 2)
        d = (dev["lon"] % 2) * 4 + dev["lev"]
        return remote(f0.at[half, d], fy.at[half, c * 4 + y], fy_s.at[half, t], fy_r.at[half, t], dev)

    def fz_copy(k):
        return remote(fs.at[k], fz.at[z], fz_s.at[k], fz_r.at[k], device(dz=NZ - offset(k)))

    lanes = pl.ds(pl.multiple_of(x * 128, 128), 128)

    def near_y(t):
        return remote(
            pack.at[0, pl.ds(0, 2)], w_kv.at[0, :, c, y, :, :, lanes], wp_s.at[0, t], wp_r.at[0, t], device(dy=t)
        )

    def near_x(t):
        ref = w_kv.at[0, :, c, :, :, :, lanes]
        return remote(ref, ref, wp_s.at[1, t], wp_r.at[1, t], device(dx=t))

    def far_x(t):
        return remote(
            pack.at[1, pl.ds(0, 2)], w_kv.at[1, :, c, y, :, :, lanes], wp_s.at[2, t], wp_r.at[2, t], device(dx=t)
        )

    def far_y(t):
        ref = w_kv.at[1, :, c, y]
        return remote(ref, ref, wp_s.at[3, t], wp_r.at[3, t], device(dy=t))

    def wq_copy(t):
        return remote(pack.at[:, 3], q_all.at[:, c, y], wy_s.at[0, t], wy_r.at[0, t], device(dy=t))

    def wy_copy(t):
        return remote(pack.at[:, 2], w_o.at[:, c, y, :, :, lanes], wy_s.at[1, t], wy_r.at[1, t], device(dy=t))

    def wx_copy(t):
        ref = w_o.at[:, c, :, :, :, lanes]
        return remote(ref, ref, wx_s.at[t], wx_r.at[t], device(dx=t))

    def wc_copy(i, side):
        ref = (w_kv.at[0, :, side], w_kv.at[1, :, side], w_o.at[:, side], q_all.at[:, side])[i]
        return remote(ref, ref, wc_s.at[i], wc_r.at[i], device(dc=1))

    def regroup(half):
        for i in range(2):
            rows = [wz[8 * half + 4 * i + j].astype(F32) for j in range(4)]
            for m, at in enumerate((4, 8, 12, 0)):
                block = jnp.concatenate([r[at : at + 4] for r in rows], axis=0).astype(BF16)
                pack[half, m, i] = block
                if m == 3:
                    q_all[half, c, y, i] = block
                elif m == 2:
                    w_o[half, c, y, i, :, lanes] = block
                else:
                    w_kv[half, m, c, y, i, :, lanes] = block

    pl.semaphore_wait(barrier, NZ - 1 + NX - 1 + 7)
    loop(1, NZ, lambda k: wz_copy(NZ - k).start())
    loop(1, 8, lambda t: fy_copy(t, 1).start())
    for load in loads[5:]:
        load.wait()
    shifted[...] = jnp.zeros_like(shifted)
    starts = (0, IN, 2 * IN - 128, 3 * IN - 128)
    for u in range(4):
        shifted[u, starts[u] : starts[u] + IN, :] = embed[...]

    def head_of(g):
        k = ((g >> 8) << 3) | ((g >> 2) & 7)
        return (z + jnp.where((k & 1) == 1, (k + 1) >> 1, NZ - (k >> 1))) & (NZ - 1)

    g = iota((D, 128), 0)
    place = (head_of(g) * 32 + ((g >> 7) & 1) * 16 + ((g >> 5) & 3) * 4 + (g & 3))[:, :1]
    natural_t[...] = one_hot(iota((D, D), 1) == place)
    ki = iota((256, D), 0) & 127
    head = head_of(iota((1, D), 1))
    for a in range(LATENT):
        spread[a] = one_hot(ki == a * HEADS + head)

    def gather_slots(half):
        for d in range(8):
            part = fy[half, d].astype(F32)
            whole[d, :, 0:512] = part
            whole[d, :, 512:] = jnp.concatenate(
                [part[12:16, 0:128], part[12:16, 128:256], part[12:16, 256:384], jnp.zeros((4, 128), F32)], axis=0
            )

    def keep(half, pick):
        kept[...] = dot(pick, whole[...].astype(BF16).reshape(128, UNITS))
        for e in range(8):
            fs[8 * half + e] = jnp.concatenate(
                [kept[16 * u : 16 * u + 16, e * IN : (e + 1) * IN] for u in range(4)] + [blank], axis=1
            ).astype(BF16)

    loop(1, 8, lambda t: fy_copy(t, 1).wait_recv())
    loop(1, 8, lambda t: fy_copy(t, 0).start())
    blank = jnp.zeros((16, 64), F32)
    at_row = iota((16, 128), 0)
    at_lane = iota((16, 128), 1)
    picks = []
    for d in range(8):
        listed = fy[1, d, :, 384:512].astype(F32)[12:13]
        level = jnp.sum(jnp.where(at_row == at_lane, listed, 0.0), axis=1, keepdims=True)
        picks.append(
            jnp.where(
                (level == (at_lane % 16).astype(F32)) & (at_row < 12)
                & (at_lane // 32 == d // 4) & (at_row % 2 == (at_lane // 16) % 2),
                1.0,
                0.0,
            )
        )
    pick = jnp.transpose(jnp.concatenate(picks, axis=0))[:64].astype(BF16)
    gather_slots(1)
    keep(1, pick)
    loop(0, 8, lambda k: fz_copy(NZ - 1 - k).start())
    loop(1, 8, lambda k: wz_copy(k).wait_recv())
    regroup(0)
    loop(1, NY, lambda t: near_y(t).start())
    loop(8, NZ, lambda k: wz_copy(k).wait_recv())
    regroup(1)
    loop(1, NX, lambda t: far_x(t).start())
    loop(1, NY, lambda t: wq_copy(t).start())
    loop(1, NY, lambda t: wy_copy(t).start())
    loop(1, 8, lambda t: fy_copy(t, 0).wait_recv())
    gather_slots(0)
    keep(0, pick)
    loop(1, 8, lambda k: fz_copy(8 - k).start())
    fz[z] = fs[0]
    loop(1, NY, lambda t: near_y(t).wait_recv())
    loop(1, NX, lambda t: near_x(t).start())
    loop(1, NX, lambda t: far_x(t).wait_recv())
    loop(1, NY, lambda t: far_y(t).start())
    loop(1, NY, lambda t: wq_copy(t).wait_recv())
    wc_copy(3, c).start()
    loop(1, NY, lambda t: wy_copy(t).wait_recv())
    loop(1, NX, lambda t: wx_copy(t).start())
    loop(1, NX, lambda t: near_x(t).wait_recv())
    wc_copy(0, c).start()

    loop(1, NZ, lambda k: fz_copy(k).wait_recv())
    r = iota((ROWS, 256), 0)
    j = iota((ROWS, 256), 1)
    rows = dot(one_hot(j == (r % 16) * 16 + r // 16), fz[...].reshape(256, 384)).astype(BF16)
    encoding = jnp.broadcast_to(encode[...].astype(F32)[:, None, :], (LEVELS, 16, D)).reshape(ROWS, D)
    for u, (lo, hi) in enumerate(((0, 128), (0, 256), (128, 256), (128, 384))):
        emb[u] = (dot(rows[:, lo:hi], shifted[u, : hi - lo, :]) + encoding).astype(BF16)

    loop(1, NY, lambda t: far_y(t).wait_recv())
    wc_copy(1, c).start()
    scale = 1.0 / math.sqrt(D // HEADS)

    def attend(half):
        g = iota((256, 128), 0) + 256 * half
        at_lane = iota((256, 128), 1)
        qv = q_all[half].astype(F32).reshape(256, 128)
        found = jnp.zeros((256, 128), F32)
        for a in range(LATENT):
            found = jnp.where(at_lane == a * HEADS + head_of(g), qv[:, a : a + 1], found)
        found = found.astype(BF16)
        k_w = w_kv[half, 0].reshape(256, D)
        v_w = w_kv[half, 1].reshape(256, D)
        cut_at = slice(256 * half, 256 * half + 256)
        rows = emb[...].reshape(4 * ROWS, D)
        keys = nt(rows, k_w).astype(BF16)
        scores = (dot(keys, found) * scale).reshape(4, LEVELS, 16, 128)
        highest = jnp.max(scores, axis=1, keepdims=True)
        expo = jnp.exp(scores - highest)
        weight = (expo * (1.0 / jnp.sum(expo, axis=1, keepdims=True))).reshape(4 * ROWS, 128)
        top = weight.astype(BF16)
        low = (weight - top.astype(F32)).astype(BF16)
        both = jnp.concatenate([top, low], axis=1)
        values = nt(rows, v_w).astype(BF16).astype(F32)
        for a in range(LATENT):
            wide = dot(both, spread[a, :, cut_at])
            total = jnp.sum((wide * values).reshape(4, LEVELS, 16, 256), axis=1)
            for u in range(4):
                mixed[a, 2 * half, pl.ds(u, 16, 4), :] = total[u, :, :128]
                mixed[a, 2 * half + 1, pl.ds(u, 16, 4), :] = total[u, :, 128:]

    wc_copy(3, 1 - c).wait_recv()
    wc_copy(0, 1 - c).wait_recv()
    attend(0)
    loop(1, NX, lambda t: wx_copy(t).wait_recv())
    wc_copy(2, c).start()
    wc_copy(1, 1 - c).wait_recv()
    attend(1)
    block = jnp.concatenate(
        [jnp.concatenate([mixed[a, i] for i in range(4)], axis=1) for a in range(LATENT)], axis=0
    ).astype(BF16)
    block = dot(block, natural_t[...]).astype(BF16)
    wc_copy(2, 1 - c).wait_recv()
    block = nt(block, w_o[...].reshape(D, D)).astype(BF16)
    out[...] = dot(block, natural_t[...]).astype(BF16).reshape(LATENT, 64, D)

    loop(1, NZ, lambda k: wz_copy(k).wait_send())
    loop(1, NZ, lambda k: fz_copy(k).wait_send())
    for half in range(2):
        loop(1, 8, lambda t: fy_copy(t, half).wait_send())
    loop(1, NY, lambda t: near_y(t).wait_send())
    loop(1, NX, lambda t: near_x(t).wait_send())
    loop(1, NX, lambda t: far_x(t).wait_send())
    loop(1, NY, lambda t: far_y(t).wait_send())
    loop(1, NY, lambda t: wq_copy(t).wait_send())
    loop(1, NY, lambda t: wy_copy(t).wait_send())
    loop(1, NX, lambda t: wx_copy(t).wait_send())
    for i in range(4):
        wc_copy(i, c).wait_send()


def encode_patches(*operands):
    dma = pltpu.SemaphoreType.DMA
    vmem = pltpu.VMEM
    fields, slot_level, latent, qkv, out_w, embed, encode = operands
    operands = [pltpu.with_memory_space_constraint(o, pltpu.HBM) for o in operands]
    return pl.pallas_call(
        kernel,
        out_shape=jax.ShapeDtypeStruct((LATENT, 64, D), BF16),
        in_specs=[pl.BlockSpec(memory_space=pltpu.HBM)] * 7,
        out_specs=pl.BlockSpec(memory_space=pltpu.VMEM),
        scratch_shapes=[
            vmem(fields.shape, BF16),
            pltpu.SMEM(slot_level.shape, jnp.int32),
            vmem(latent.shape, BF16),
            vmem(qkv.shape, BF16),
            vmem(out_w.shape, BF16),
            vmem(embed.shape, BF16),
            vmem(encode.shape, BF16),
            vmem((NX, 16, 128), BF16),
            vmem((NZ, 16, 128), BF16),
            vmem((2, 4, 2, 16, 128), BF16),
            vmem((2, 2, NC, NY, 2, 16, D), BF16),
            vmem((2, NC, NY, 2, 16, D), BF16),
            vmem((2, NC, NY, 2, 16, 128), BF16),
            vmem((2, 8, 16, 512), BF16),
            vmem((2, 8, 16, 512), BF16),
            vmem((8, 16, UNITS), F32),
            vmem((64, UNITS), F32),
            vmem((NZ, 16, 384), BF16),
            vmem((NZ, 16, 384), BF16),
            vmem((4, 256, D), BF16),
            vmem((4, ROWS, D), BF16),
            vmem((LATENT, 256, D), BF16),
            vmem((D, D), BF16),
            vmem((LATENT, 4, 64, 128), F32),
            dma((7,)),
            dma((NZ,)), dma((NZ,)),
            dma((4, 4)), dma((4, 4)),
            dma((2, NY)), dma((2, NY)),
            dma((NX,)), dma((NX,)),
            dma((4,)), dma((4,)),
            dma((2, 8)), dma((2, 8)),
            dma((NZ,)), dma((NZ,)),
        ],
        compiler_params=pltpu.CompilerParams(
            collective_id=0, has_side_effects=True, vmem_limit_bytes=VMEM_LIMIT
        ),
        cost_estimate=pl.CostEstimate(flops=3 * 10**9, bytes_accessed=10**6, transcendentals=10**5),
        name="encode_patches",
    )(*operands)


def on_device(fields, slot_level, embed_weight, level_encoding, latent_queries, qkv_weight, out_weight):
    out = encode_patches(
        fields, slot_level, latent_queries, qkv_weight, out_weight, embed_weight, level_encoding
    )
    return out.reshape(LATENT, 1, 64, D)


def solution(mesh):
    in_specs = (
        P("lev", "lon", "lat"),
        P("lev"),
        P(),
        P(),
        P(),
        P(None, ("lon", "lev"), None),
        P(("lon", "lev"), None),
    )
    out_specs = P(None, ("lat", "lon", "lev"), None, None)
    return jax.shard_map(
        on_device, mesh=mesh, in_specs=in_specs, out_specs=out_specs, check_vma=False
    )
```

```python
import math

import jax
import jax.numpy as jnp
from jax import lax
from jax.experimental import pallas as pl
from jax.experimental.pallas import tpu as pltpu
from jax.sharding import PartitionSpec as P

MESH = pl.DeviceIdType.MESH
F32 = jnp.float32
BF16 = jnp.bfloat16
NZ, NY, NX, NC = 16, 4, 4, 2
IN = 80
D = 512
LEVELS = 14
HEADS = 16
LATENT = 3
UNITS = 8 * IN
ROWS = LEVELS * 16
VMEM_LIMIT = 40 * 1024 * 1024


def iota(shape, dim):
    return lax.broadcasted_iota(jnp.int32, shape, dim)


def one_hot(mask):
    return jnp.where(mask, 1.0, 0.0).astype(BF16)


def dot(a, b):
    return jnp.dot(a, b, preferred_element_type=F32)


def nt(a, b):
    return lax.dot_general(a, b, (((1,), (1,)), ((), ())), preferred_element_type=F32)


def offset(k):
    return (NZ + (k % 2) * ((k + 1) // 2) - (1 - k % 2) * (k // 2)) % NZ


def loop(lo, hi, act):
    def body(t, carry):
        act(t)
        return carry

    lax.fori_loop(lo, hi, body, 0)


def kernel(
    fields_h, slot_h, latent_h, qkv_h, out_w_h, embed_h, encode_h,
    out,
    fields, slot_level, latent, qkv, out_w, embed, encode,
    tile, wz, pack, w_kv, w_o, q_all, f0, fy, whole, kept, fs, fz,
    shifted, emb, spread, natural_t, mixed,
    in_s, wz_s, wz_r, wp_s, wp_r, wy_s, wy_r, wx_s, wx_r, wc_s, wc_r, fy_s, fy_r, fz_s, fz_r,
):
    x = lax.axis_index("lat")
    lon = lax.axis_index("lon")
    y = lax.axis_index("lev")
    z = lon // 2
    c = lon % 2

    def device(dx=0, dy=0, dz=0, dc=0):
        return {
            "lat": (x + dx) % NX,
            "lon": ((z + dz) % NZ) * 2 + (c + dc) % 2,
            "lev": (y + dy) % NY,
        }

    barrier = pltpu.get_barrier_semaphore()

    def greet(dev):
        pl.semaphore_signal(barrier, inc=1, device_id=dev, device_id_type=MESH)

    loop(1, NZ, lambda k: greet(device(dz=offset(NZ - k))))
    loop(1, NX, lambda t: greet(device(dx=t)))
    loop(1, 8, lambda t: greet(device(dy=t // 2, dc=t % 2)))

    loads = [
        pltpu.make_async_copy(src, dst, in_s.at[i])
        for i, (src, dst) in enumerate(
            (
                (qkv_h, qkv), (out_w_h, out_w), (latent_h, latent), (slot_h, slot_level),
                (fields_h, fields), (embed_h, embed), (encode_h, encode),
            )
        )
    ]
    for load in loads:
        load.start()
    for load in loads[:3]:
        load.wait()

    wq = qkv[0].astype(F32)
    lat = latent[...].astype(F32)
    lane = iota((4, 128), 1)
    q = jnp.zeros((4, 128), F32)
    for a in range(LATENT):
        col = jnp.sum(wq * lat[a : a + 1, :], axis=1, keepdims=True)
        q = jnp.where(lane == a, col, q)
    for part in range(NX):
        cut_at = slice(part * 128, part * 128 + 128)
        tile[part] = jnp.concatenate(
            [q, qkv[1, :, cut_at].astype(F32), qkv[2, :, cut_at].astype(F32), out_w[:, cut_at].astype(F32)],
            axis=0,
        ).astype(BF16)
    wz[0] = tile[x]

    for load in loads[3:5]:
        load.wait()
    at_row = iota((4, 128), 0)
    slot_of_lane = iota((4, 128), 1) // 2
    levels = jnp.full((4, 128), -1.0, F32)
    for s in range(6):
        levels = jnp.where(slot_of_lane == s, slot_level[s].astype(F32), levels)
    for half in (1, 0):
        blocks = []
        for e in range(8):
            to = (z + NZ - offset(8 * half + e)) % NZ
            at = pl.ds(pl.multiple_of(to * UNITS, 128), UNITS)
            blocks.append(jnp.concatenate([fields[s, :, at].astype(F32) for s in range(6)], axis=0))
        for d in range(8):
            units = jnp.concatenate([blocks[e][:, d * IN : (d + 1) * IN] for e in range(8)], axis=1)
            last = units[:, 512:]
            spare = jnp.concatenate([last[0:4], last[4:8], last[8:12], levels], axis=1)
            f0[half, d] = jnp.concatenate([units[:, :512], spare], axis=0).astype(BF16)
    for half in range(2):
        fy[half, c * 4 + y] = f0[half, c * 4 + y]

    def remote(src, dst, send, recv, dev):
        return pltpu.make_async_remote_copy(
            src_ref=src, dst_ref=dst, send_sem=send, recv_sem=recv, device_id=dev, device_id_type=MESH
        )

    def wz_copy(k):
        return remote(tile.at[x], wz.at[k], wz_s.at[k], wz_r.at[k], device(dz=NZ - offset(k)))

    def fy_copy(t, half):
        dev = device(dy=t // 2, dc=t % 2)
        d = (dev["lon"] % 2) * 4 + dev["lev"]
        return remote(f0.at[half, d], fy.at[half, c * 4 + y], fy_s.at[half, t], fy_r.at[half, t], dev)

    def fz_copy(k):
        return remote(fs.at[k], fz.at[z], fz_s.at[k], fz_r.at[k], device(dz=NZ - offset(k)))

    lanes = pl.ds(pl.multiple_of(x * 128, 128), 128)

    def near_y(t):
        return remote(
            pack.at[0, pl.ds(0, 2)], w_kv.at[0, :, c, y, :, :, lanes], wp_s.at[0, t], wp_r.at[0, t], device(dy=t)
        )

    def near_x(t):
        ref = w_kv.at[0, :, c, :, :, :, lanes]
        return remote(ref, ref, wp_s.at[1, t], wp_r.at[1, t], device(dx=t))

    def far_x(t):
        return remote(
            pack.at[1, pl.ds(0, 2)], w_kv.at[1, :, c, y, :, :, lanes], wp_s.at[2, t], wp_r.at[2, t], device(dx=t)
        )

    def far_y(t):
        ref = w_kv.at[1, :, c, y]
        return remote(ref, ref, wp_s.at[3, t], wp_r.at[3, t], device(dy=t))

    def wq_copy(t):
        return remote(pack.at[:, 3], q_all.at[:, c, y], wy_s.at[0, t], wy_r.at[0, t], device(dy=t))

    def wy_copy(t):
        return remote(pack.at[:, 2], w_o.at[:, c, y, :, :, lanes], wy_s.at[1, t], wy_r.at[1, t], device(dy=t))

    def wx_copy(t):
        ref = w_o.at[:, c, :, :, :, lanes]
        return remote(ref, ref, wx_s.at[t], wx_r.at[t], device(dx=t))

    def wc_copy(i, side):
        ref = (w_kv.at[0, :, side], w_kv.at[1, :, side], w_o.at[:, side], q_all.at[:, side])[i]
        return remote(ref, ref, wc_s.at[i], wc_r.at[i], device(dc=1))

    def regroup(half):
        for i in range(2):
            rows = [wz[8 * half + 4 * i + j].astype(F32) for j in range(4)]
            for m, at in enumerate((4, 8, 12, 0)):
                block = jnp.concatenate([r[at : at + 4] for r in rows], axis=0).astype(BF16)
                pack[half, m, i] = block
                if m == 3:
                    q_all[half, c, y, i] = block
                elif m == 2:
                    w_o[half, c, y, i, :, lanes] = block
                else:
                    w_kv[half, m, c, y, i, :, lanes] = block

    pl.semaphore_wait(barrier, NZ - 1 + NX - 1 + 7)
    loop(1, NZ, lambda k: wz_copy(NZ - k).start())
    loop(1, 8, lambda t: fy_copy(t, 1).start())
    for load in loads[5:]:
        load.wait()
    shifted[...] = jnp.zeros_like(shifted)
    starts = (0, IN, 2 * IN - 128, 3 * IN - 128)
    for u in range(4):
        shifted[u, starts[u] : starts[u] + IN, :] = embed[...]

    def head_of(g):
        k = ((g >> 8) << 3) | ((g >> 2) & 7)
        return (z + jnp.where((k & 1) == 1, (k + 1) >> 1, NZ - (k >> 1))) & (NZ - 1)

    g = iota((D, 128), 0)
    place = (head_of(g) * 32 + ((g >> 7) & 1) * 16 + ((g >> 5) & 3) * 4 + (g & 3))[:, :1]
    natural_t[...] = one_hot(iota((D, D), 1) == place)
    ki = iota((256, D), 0) & 127
    head = head_of(iota((1, D), 1))
    for a in range(LATENT):
        spread[a] = one_hot(ki == a * HEADS + head)

    def gather_slots(half):
        for d in range(8):
            part = fy[half, d].astype(F32)
            whole[d, :, 0:512] = part
            whole[d, :, 512:] = jnp.concatenate(
                [part[12:16, 0:128], part[12:16, 128:256], part[12:16, 256:384], jnp.zeros((4, 128), F32)], axis=0
            )

    def keep(half, pick):
        kept[...] = dot(pick, whole[...].astype(BF16).reshape(128, UNITS))
        for e in range(8):
            fs[8 * half + e] = jnp.concatenate(
                [kept[16 * u : 16 * u + 16, e * IN : (e + 1) * IN] for u in range(4)] + [blank], axis=1
            ).astype(BF16)

    loop(1, 8, lambda k: wz_copy(k).wait_recv())
    regroup(0)
    loop(1, NY, lambda t: near_y(t).start())
    loop(1, 8, lambda t: fy_copy(t, 1).wait_recv())
    loop(1, 8, lambda t: fy_copy(t, 0).start())
    blank = jnp.zeros((16, 64), F32)
    at_row = iota((16, 128), 0)
    at_lane = iota((16, 128), 1)
    picks = []
    for d in range(8):
        listed = fy[1, d, :, 384:512].astype(F32)[12:13]
        level = jnp.sum(jnp.where(at_row == at_lane, listed, 0.0), axis=1, keepdims=True)
        picks.append(
            jnp.where(
                (level == (at_lane % 16).astype(F32)) & (at_row < 12)
                & (at_lane // 32 == d // 4) & (at_row % 2 == (at_lane // 16) % 2),
                1.0,
                0.0,
            )
        )
    pick = jnp.transpose(jnp.concatenate(picks, axis=0))[:64].astype(BF16)
    gather_slots(1)
    keep(1, pick)
    loop(0, 8, lambda k: fz_copy(NZ - 1 - k).start())
    loop(8, NZ, lambda k: wz_copy(k).wait_recv())
    regroup(1)
    loop(1, NX, lambda t: far_x(t).start())
    loop(1, NY, lambda t: wq_copy(t).start())
    loop(1, NY, lambda t: wy_copy(t).start())
    loop(1, NY, lambda t: near_y(t).wait_recv())
    loop(1, NX, lambda t: near_x(t).start())
    loop(1, 8, lambda t: fy_copy(t, 0).wait_recv())
    gather_slots(0)
    keep(0, pick)
    loop(1, 8, lambda k: fz_copy(8 - k).start())
    fz[z] = fs[0]
    loop(1, NX, lambda t: far_x(t).wait_recv())
    loop(1, NY, lambda t: far_y(t).start())
    loop(1, NY, lambda t: wq_copy(t).wait_recv())
    wc_copy(3, c).start()
    loop(1, NY, lambda t: wy_copy(t).wait_recv())
    loop(1, NX, lambda t: wx_copy(t).start())
    loop(1, NX, lambda t: near_x(t).wait_recv())
    wc_copy(0, c).start()

    loop(1, NY, lambda t: far_y(t).wait_recv())
    wc_copy(1, c).start()
    loop(1, NZ, lambda k: fz_copy(k).wait_recv())
    r = iota((ROWS, 256), 0)
    j = iota((ROWS, 256), 1)
    rows = dot(one_hot(j == (r % 16) * 16 + r // 16), fz[...].reshape(256, 384)).astype(BF16)
    encoding = jnp.broadcast_to(encode[...].astype(F32)[:, None, :], (LEVELS, 16, D)).reshape(ROWS, D)
    for u, (lo, hi) in enumerate(((0, 128), (0, 256), (128, 256), (128, 384))):
        emb[u] = (dot(rows[:, lo:hi], shifted[u, : hi - lo, :]) + encoding).astype(BF16)

    scale = 1.0 / math.sqrt(D // HEADS)

    def attend(half):
        g = iota((256, 128), 0) + 256 * half
        at_lane = iota((256, 128), 1)
        qv = q_all[half].astype(F32).reshape(256, 128)
        found = jnp.zeros((256, 128), F32)
        for a in range(LATENT):
            found = jnp.where(at_lane == a * HEADS + head_of(g), qv[:, a : a + 1], found)
        found = found.astype(BF16)
        k_w = w_kv[half, 0].reshape(256, D)
        v_w = w_kv[half, 1].reshape(256, D)
        cut_at = slice(256 * half, 256 * half + 256)
        rows = emb[...].reshape(4 * ROWS, D)
        keys = nt(rows, k_w).astype(BF16)
        scores = (dot(keys, found) * scale).reshape(4, LEVELS, 16, 128)
        highest = jnp.max(scores, axis=1, keepdims=True)
        expo = jnp.exp(scores - highest)
        weight = (expo * (1.0 / jnp.sum(expo, axis=1, keepdims=True))).reshape(4 * ROWS, 128)
        top = weight.astype(BF16)
        low = (weight - top.astype(F32)).astype(BF16)
        both = jnp.concatenate([top, low], axis=1)
        values = nt(rows, v_w).astype(BF16).astype(F32)
        for a in range(LATENT):
            wide = dot(both, spread[a, :, cut_at])
            total = jnp.sum((wide * values).reshape(4, LEVELS, 16, 256), axis=1)
            for u in range(4):
                mixed[a, 2 * half, pl.ds(u, 16, 4), :] = total[u, :, :128]
                mixed[a, 2 * half + 1, pl.ds(u, 16, 4), :] = total[u, :, 128:]

    wc_copy(3, 1 - c).wait_recv()
    wc_copy(0, 1 - c).wait_recv()
    attend(0)
    loop(1, NX, lambda t: wx_copy(t).wait_recv())
    wc_copy(2, c).start()
    wc_copy(1, 1 - c).wait_recv()
    attend(1)
    block = jnp.concatenate(
        [jnp.concatenate([mixed[a, i] for i in range(4)], axis=1) for a in range(LATENT)], axis=0
    ).astype(BF16)
    block = dot(block, natural_t[...]).astype(BF16)
    wc_copy(2, 1 - c).wait_recv()
    block = nt(block, w_o[...].reshape(D, D)).astype(BF16)
    out[...] = dot(block, natural_t[...]).astype(BF16).reshape(LATENT, 64, D)

    loop(1, NZ, lambda k: wz_copy(k).wait_send())
    loop(1, NZ, lambda k: fz_copy(k).wait_send())
    for half in range(2):
        loop(1, 8, lambda t: fy_copy(t, half).wait_send())
    loop(1, NY, lambda t: near_y(t).wait_send())
    loop(1, NX, lambda t: near_x(t).wait_send())
    loop(1, NX, lambda t: far_x(t).wait_send())
    loop(1, NY, lambda t: far_y(t).wait_send())
    loop(1, NY, lambda t: wq_copy(t).wait_send())
    loop(1, NY, lambda t: wy_copy(t).wait_send())
    loop(1, NX, lambda t: wx_copy(t).wait_send())
    for i in range(4):
        wc_copy(i, c).wait_send()


def encode_patches(*operands):
    dma = pltpu.SemaphoreType.DMA
    vmem = pltpu.VMEM
    fields, slot_level, latent, qkv, out_w, embed, encode = operands
    operands = [pltpu.with_memory_space_constraint(o, pltpu.HBM) for o in operands]
    return pl.pallas_call(
        kernel,
        out_shape=jax.ShapeDtypeStruct((LATENT, 64, D), BF16),
        in_specs=[pl.BlockSpec(memory_space=pltpu.HBM)] * 7,
        out_specs=pl.BlockSpec(memory_space=pltpu.VMEM),
        scratch_shapes=[
            vmem(fields.shape, BF16),
            pltpu.SMEM(slot_level.shape, jnp.int32),
            vmem(latent.shape, BF16),
            vmem(qkv.shape, BF16),
            vmem(out_w.shape, BF16),
            vmem(embed.shape, BF16),
            vmem(encode.shape, BF16),
            vmem((NX, 16, 128), BF16),
            vmem((NZ, 16, 128), BF16),
            vmem((2, 4, 2, 16, 128), BF16),
            vmem((2, 2, NC, NY, 2, 16, D), BF16),
            vmem((2, NC, NY, 2, 16, D), BF16),
            vmem((2, NC, NY, 2, 16, 128), BF16),
            vmem((2, 8, 16, 512), BF16),
            vmem((2, 8, 16, 512), BF16),
            vmem((8, 16, UNITS), F32),
            vmem((64, UNITS), F32),
            vmem((NZ, 16, 384), BF16),
            vmem((NZ, 16, 384), BF16),
            vmem((4, 256, D), BF16),
            vmem((4, ROWS, D), BF16),
            vmem((LATENT, 256, D), BF16),
            vmem((D, D), BF16),
            vmem((LATENT, 4, 64, 128), F32),
            dma((7,)),
            dma((NZ,)), dma((NZ,)),
            dma((4, 4)), dma((4, 4)),
            dma((2, NY)), dma((2, NY)),
            dma((NX,)), dma((NX,)),
            dma((4,)), dma((4,)),
            dma((2, 8)), dma((2, 8)),
            dma((NZ,)), dma((NZ,)),
        ],
        compiler_params=pltpu.CompilerParams(
            collective_id=0, has_side_effects=True, vmem_limit_bytes=VMEM_LIMIT
        ),
        cost_estimate=pl.CostEstimate(flops=3 * 10**9, bytes_accessed=10**6, transcendentals=10**5),
        name="encode_patches",
    )(*operands)


def on_device(fields, slot_level, embed_weight, level_encoding, latent_queries, qkv_weight, out_weight):
    out = encode_patches(
        fields, slot_level, latent_queries, qkv_weight, out_weight, embed_weight, level_encoding
    )
    return out.reshape(LATENT, 1, 64, D)


def solution(mesh):
    in_specs = (
        P("lev", "lon", "lat"),
        P("lev"),
        P(),
        P(),
        P(),
        P(None, ("lon", "lev"), None),
        P(("lon", "lev"), None),
    )
    out_specs = P(None, ("lat", "lon", "lev"), None, None)
    return jax.shard_map(
        on_device, mesh=mesh, in_specs=in_specs, out_specs=out_specs, check_vma=False
    )
```

```python
import math

import jax
import jax.numpy as jnp
from jax import lax
from jax.experimental import pallas as pl
from jax.experimental.pallas import tpu as pltpu
from jax.sharding import PartitionSpec as P

MESH = pl.DeviceIdType.MESH
F32 = jnp.float32
BF16 = jnp.bfloat16
NZ, NY, NX, NC = 16, 4, 4, 2
IN = 80
D = 512
LEVELS = 14
HEADS = 16
LATENT = 3
UNITS = 8 * IN
ROWS = LEVELS * 16
VMEM_LIMIT = 40 * 1024 * 1024


def iota(shape, dim):
    return lax.broadcasted_iota(jnp.int32, shape, dim)


def one_hot(mask):
    return jnp.where(mask, 1.0, 0.0).astype(BF16)


def dot(a, b):
    return jnp.dot(a, b, preferred_element_type=F32)


def nt(a, b):
    return lax.dot_general(a, b, (((1,), (1,)), ((), ())), preferred_element_type=F32)


def offset(k):
    return (NZ + (k % 2) * ((k + 1) // 2) - (1 - k % 2) * (k // 2)) % NZ


def loop(lo, hi, act):
    def body(t, carry):
        act(t)
        return carry

    lax.fori_loop(lo, hi, body, 0)


def kernel(
    fields_h, slot_h, latent_h, qkv_h, out_w_h, embed_h, encode_h,
    out,
    fields, slot_level, latent, qkv, out_w, embed, encode,
    tile, wz, pack, w_kv, w_o, q_all, f0, fy, whole, kept, fs, fz,
    shifted, emb, spread, natural_t, mixed,
    in_s, wz_s, wz_r, wp_s, wp_r, wy_s, wy_r, wx_s, wx_r, wc_s, wc_r, fy_s, fy_r, fz_s, fz_r,
):
    x = lax.axis_index("lat")
    lon = lax.axis_index("lon")
    y = lax.axis_index("lev")
    z = lon // 2
    c = lon % 2

    def device(dx=0, dy=0, dz=0, dc=0):
        return {
            "lat": (x + dx) % NX,
            "lon": ((z + dz) % NZ) * 2 + (c + dc) % 2,
            "lev": (y + dy) % NY,
        }

    barrier = pltpu.get_barrier_semaphore()

    def greet(dev):
        pl.semaphore_signal(barrier, inc=1, device_id=dev, device_id_type=MESH)

    loop(1, NZ, lambda k: greet(device(dz=offset(NZ - k))))
    loop(1, NX, lambda t: greet(device(dx=t)))
    loop(1, 8, lambda t: greet(device(dy=t // 2, dc=t % 2)))

    loads = [
        pltpu.make_async_copy(src, dst, in_s.at[i])
        for i, (src, dst) in enumerate(
            (
                (qkv_h, qkv), (out_w_h, out_w), (latent_h, latent), (slot_h, slot_level),
                (fields_h, fields), (embed_h, embed), (encode_h, encode),
            )
        )
    ]
    for load in loads:
        load.start()
    for load in loads[:3]:
        load.wait()

    wq = qkv[0].astype(F32)
    lat = latent[...].astype(F32)
    lane = iota((4, 128), 1)
    q = jnp.zeros((4, 128), F32)
    for a in range(LATENT):
        col = jnp.sum(wq * lat[a : a + 1, :], axis=1, keepdims=True)
        q = jnp.where(lane == a, col, q)
    for part in range(NX):
        cut_at = slice(part * 128, part * 128 + 128)
        tile[part] = jnp.concatenate(
            [q, qkv[1, :, cut_at].astype(F32), qkv[2, :, cut_at].astype(F32), out_w[:, cut_at].astype(F32)],
            axis=0,
        ).astype(BF16)
    wz[0] = tile[x]

    for load in loads[3:5]:
        load.wait()
    at_row = iota((4, 128), 0)
    slot_of_lane = iota((4, 128), 1) // 2
    levels = jnp.full((4, 128), -1.0, F32)
    for s in range(6):
        levels = jnp.where(slot_of_lane == s, slot_level[s].astype(F32), levels)
    for half in (1, 0):
        blocks = []
        for e in range(8):
            to = (z + NZ - offset(8 * half + e)) % NZ
            at = pl.ds(pl.multiple_of(to * UNITS, 128), UNITS)
            blocks.append(jnp.concatenate([fields[s, :, at].astype(F32) for s in range(6)], axis=0))
        for d in range(8):
            units = jnp.concatenate([blocks[e][:, d * IN : (d + 1) * IN] for e in range(8)], axis=1)
            last = units[:, 512:]
            spare = jnp.concatenate([last[0:4], last[4:8], last[8:12], levels], axis=1)
            f0[half, d] = jnp.concatenate([units[:, :512], spare], axis=0).astype(BF16)
    for half in range(2):
        fy[half, c * 4 + y] = f0[half, c * 4 + y]

    def remote(src, dst, send, recv, dev):
        return pltpu.make_async_remote_copy(
            src_ref=src, dst_ref=dst, send_sem=send, recv_sem=recv, device_id=dev, device_id_type=MESH
        )

    def wz_copy(k):
        return remote(tile.at[x], wz.at[k], wz_s.at[k], wz_r.at[k], device(dz=NZ - offset(k)))

    def fy_copy(t, half):
        dev = device(dy=t // 2, dc=t % 2)
        d = (dev["lon"] % 2) * 4 + dev["lev"]
        return remote(f0.at[half, d], fy.at[half, c * 4 + y], fy_s.at[half, t], fy_r.at[half, t], dev)

    def fz_copy(k):
        return remote(fs.at[k], fz.at[z], fz_s.at[k], fz_r.at[k], device(dz=NZ - offset(k)))

    lanes = pl.ds(pl.multiple_of(x * 128, 128), 128)

    def near_y(t):
        return remote(
            pack.at[0, pl.ds(0, 2)], w_kv.at[0, :, c, y, :, :, lanes], wp_s.at[0, t], wp_r.at[0, t], device(dy=t)
        )

    def near_x(t):
        ref = w_kv.at[0, :, c, :, :, :, lanes]
        return remote(ref, ref, wp_s.at[1, t], wp_r.at[1, t], device(dx=t))

    def far_x(t):
        return remote(
            pack.at[1, pl.ds(0, 2)], w_kv.at[1, :, c, y, :, :, lanes], wp_s.at[2, t], wp_r.at[2, t], device(dx=t)
        )

    def far_y(t):
        ref = w_kv.at[1, :, c, y]
        return remote(ref, ref, wp_s.at[3, t], wp_r.at[3, t], device(dy=t))

    def wq_copy(t):
        return remote(pack.at[:, 3], q_all.at[:, c, y], wy_s.at[0, t], wy_r.at[0, t], device(dy=t))

    def wy_copy(t):
        return remote(pack.at[:, 2], w_o.at[:, c, y, :, :, lanes], wy_s.at[1, t], wy_r.at[1, t], device(dy=t))

    def wx_copy(t):
        ref = w_o.at[:, c, :, :, :, lanes]
        return remote(ref, ref, wx_s.at[t], wx_r.at[t], device(dx=t))

    def wc_copy(i, side):
        ref = (w_kv.at[0, :, side], w_kv.at[1, :, side], w_o.at[:, side], q_all.at[:, side])[i]
        return remote(ref, ref, wc_s.at[i], wc_r.at[i], device(dc=1))

    def regroup(half):
        for i in range(2):
            rows = [wz[8 * half + 4 * i + j].astype(F32) for j in range(4)]
            for m, at in enumerate((4, 8, 12, 0)):
                block = jnp.concatenate([r[at : at + 4] for r in rows], axis=0).astype(BF16)
                pack[half, m, i] = block
                if m == 3:
                    q_all[half, c, y, i] = block
                elif m == 2:
                    w_o[half, c, y, i, :, lanes] = block
                else:
                    w_kv[half, m, c, y, i, :, lanes] = block

    pl.semaphore_wait(barrier, NZ - 1 + NX - 1 + 7)
    loop(1, NZ, lambda k: wz_copy(NZ - k).start())
    loop(1, 8, lambda t: fy_copy(t, 1).start())
    for load in loads[5:]:
        load.wait()
    shifted[...] = jnp.zeros_like(shifted)
    starts = (0, IN, 2 * IN - 128, 3 * IN - 128)
    for u in range(4):
        shifted[u, starts[u] : starts[u] + IN, :] = embed[...]

    def head_of(g):
        k = ((g >> 8) << 3) | ((g >> 2) & 7)
        return (z + jnp.where((k & 1) == 1, (k + 1) >> 1, NZ - (k >> 1))) & (NZ - 1)

    g = iota((D, 128), 0)
    place = (head_of(g) * 32 + ((g >> 7) & 1) * 16 + ((g >> 5) & 3) * 4 + (g & 3))[:, :1]
    natural_t[...] = one_hot(iota((D, D), 1) == place)
    ki = iota((256, D), 0) & 127
    head = head_of(iota((1, D), 1))
    for a in range(LATENT):
        spread[a] = one_hot(ki == a * HEADS + head)

    def gather_slots(half):
        for d in range(8):
            part = fy[half, d].astype(F32)
            whole[d, :, 0:512] = part
            whole[d, :, 512:] = jnp.concatenate(
                [part[12:16, 0:128], part[12:16, 128:256], part[12:16, 256:384], jnp.zeros((4, 128), F32)], axis=0
            )

    def keep(half, pick):
        kept[...] = dot(pick, whole[...].astype(BF16).reshape(128, UNITS))
        for e in range(8):
            fs[8 * half + e] = jnp.concatenate(
                [kept[16 * u : 16 * u + 16, e * IN : (e + 1) * IN] for u in range(4)] + [blank], axis=1
            ).astype(BF16)

    loop(1, 8, lambda k: wz_copy(k).wait_recv())
    regroup(0)
    loop(1, NY, lambda t: near_y(t).start())
    loop(1, 8, lambda t: fy_copy(t, 1).wait_recv())
    loop(1, 8, lambda t: fy_copy(t, 0).start())
    blank = jnp.zeros((16, 64), F32)
    at_row = iota((16, 128), 0)
    at_lane = iota((16, 128), 1)
    picks = []
    for d in range(8):
        listed = fy[1, d, :, 384:512].astype(F32)[12:13]
        level = jnp.sum(jnp.where(at_row == at_lane, listed, 0.0), axis=1, keepdims=True)
        picks.append(
            jnp.where(
                (level == (at_lane % 16).astype(F32)) & (at_row < 12)
                & (at_lane // 32 == d // 4) & (at_row % 2 == (at_lane // 16) % 2),
                1.0,
                0.0,
            )
        )
    pick = jnp.transpose(jnp.concatenate(picks, axis=0))[:64].astype(BF16)
    gather_slots(1)
    keep(1, pick)
    loop(0, 8, lambda k: fz_copy(NZ - 1 - k).start())
    loop(8, NZ, lambda k: wz_copy(k).wait_recv())
    regroup(1)
    loop(1, NX, lambda t: far_x(t).start())
    loop(1, NY, lambda t: wq_copy(t).start())
    loop(1, NY, lambda t: wy_copy(t).start())
    loop(1, NY, lambda t: near_y(t).wait_recv())
    loop(1, NX, lambda t: near_x(t).start())
    loop(1, 8, lambda t: fy_copy(t, 0).wait_recv())
    gather_slots(0)
    keep(0, pick)
    loop(1, 8, lambda k: fz_copy(8 - k).start())
    fz[z] = fs[0]
    loop(1, NX, lambda t: far_x(t).wait_recv())
    loop(1, NY, lambda t: far_y(t).start())
    loop(1, NY, lambda t: wq_copy(t).wait_recv())
    wc_copy(3, c).start()
    loop(1, NY, lambda t: wy_copy(t).wait_recv())
    loop(1, NX, lambda t: wx_copy(t).start())
    loop(1, NX, lambda t: near_x(t).wait_recv())
    wc_copy(0, c).start()

    loop(1, NY, lambda t: far_y(t).wait_recv())
    wc_copy(1, c).start()
    loop(1, NZ, lambda k: fz_copy(k).wait_recv())
    r = iota((ROWS, 256), 0)
    j = iota((ROWS, 256), 1)
    rows = dot(one_hot(j == (r % 16) * 16 + r // 16), fz[...].reshape(256, 384)).astype(BF16)
    encoding = jnp.broadcast_to(encode[...].astype(F32)[:, None, :], (LEVELS, 16, D)).reshape(ROWS, D)
    for u, (lo, hi) in enumerate(((0, 128), (0, 256), (128, 256), (128, 384))):
        emb[u] = (dot(rows[:, lo:hi], shifted[u, : hi - lo, :]) + encoding).astype(BF16)

    scale = 1.0 / math.sqrt(D // HEADS)

    def attend(half):
        g = iota((256, 128), 0) + 256 * half
        at_lane = iota((256, 128), 1)
        qv = q_all[half].astype(F32).reshape(256, 128)
        found = jnp.zeros((256, 128), F32)
        for a in range(LATENT):
            found = jnp.where(at_lane == a * HEADS + head_of(g), qv[:, a : a + 1], found)
        found = found.astype(BF16)
        k_w = w_kv[half, 0].reshape(256, D)
        v_w = w_kv[half, 1].reshape(256, D)
        cut_at = slice(256 * half, 256 * half + 256)
        rows = emb[...].reshape(4 * ROWS, D)
        keys = nt(rows, k_w).astype(BF16)
        scores = (dot(keys, found) * scale).reshape(4, LEVELS, 16, 128)
        highest = jnp.max(scores, axis=1, keepdims=True)
        expo = jnp.exp(scores - highest)
        weight = (expo * (1.0 / jnp.sum(expo, axis=1, keepdims=True))).reshape(4 * ROWS, 128)
        top = weight.astype(BF16)
        low = (weight - top.astype(F32)).astype(BF16)
        both = jnp.concatenate([top, low], axis=1)
        values = nt(rows, v_w).astype(BF16).astype(F32)
        for a in range(LATENT):
            wide = dot(both, spread[a, :, cut_at])
            total = jnp.sum((wide * values).reshape(4, LEVELS, 16, 256), axis=1)
            for u in range(4):
                mixed[a, 2 * half, pl.ds(u, 16, 4), :] = total[u, :, :128]
                mixed[a, 2 * half + 1, pl.ds(u, 16, 4), :] = total[u, :, 128:]

    loop(1, NX, lambda t: wx_copy(t).wait_recv())
    wc_copy(2, c).start()
    wc_copy(3, 1 - c).wait_recv()
    wc_copy(0, 1 - c).wait_recv()
    attend(0)
    wc_copy(1, 1 - c).wait_recv()
    attend(1)
    block = jnp.concatenate(
        [jnp.concatenate([mixed[a, i] for i in range(4)], axis=1) for a in range(LATENT)], axis=0
    ).astype(BF16)
    block = dot(block, natural_t[...]).astype(BF16)
    wc_copy(2, 1 - c).wait_recv()
    block = nt(block, w_o[...].reshape(D, D)).astype(BF16)
    out[...] = dot(block, natural_t[...]).astype(BF16).reshape(LATENT, 64, D)

    loop(1, NZ, lambda k: wz_copy(k).wait_send())
    loop(1, NZ, lambda k: fz_copy(k).wait_send())
    for half in range(2):
        loop(1, 8, lambda t: fy_copy(t, half).wait_send())
    loop(1, NY, lambda t: near_y(t).wait_send())
    loop(1, NX, lambda t: near_x(t).wait_send())
    loop(1, NX, lambda t: far_x(t).wait_send())
    loop(1, NY, lambda t: far_y(t).wait_send())
    loop(1, NY, lambda t: wq_copy(t).wait_send())
    loop(1, NY, lambda t: wy_copy(t).wait_send())
    loop(1, NX, lambda t: wx_copy(t).wait_send())
    for i in range(4):
        wc_copy(i, c).wait_send()


def encode_patches(*operands):
    dma = pltpu.SemaphoreType.DMA
    vmem = pltpu.VMEM
    fields, slot_level, latent, qkv, out_w, embed, encode = operands
    operands = [pltpu.with_memory_space_constraint(o, pltpu.HBM) for o in operands]
    return pl.pallas_call(
        kernel,
        out_shape=jax.ShapeDtypeStruct((LATENT, 64, D), BF16),
        in_specs=[pl.BlockSpec(memory_space=pltpu.HBM)] * 7,
        out_specs=pl.BlockSpec(memory_space=pltpu.VMEM),
        scratch_shapes=[
            vmem(fields.shape, BF16),
            pltpu.SMEM(slot_level.shape, jnp.int32),
            vmem(latent.shape, BF16),
            vmem(qkv.shape, BF16),
            vmem(out_w.shape, BF16),
            vmem(embed.shape, BF16),
            vmem(encode.shape, BF16),
            vmem((NX, 16, 128), BF16),
            vmem((NZ, 16, 128), BF16),
            vmem((2, 4, 2, 16, 128), BF16),
            vmem((2, 2, NC, NY, 2, 16, D), BF16),
            vmem((2, NC, NY, 2, 16, D), BF16),
            vmem((2, NC, NY, 2, 16, 128), BF16),
            vmem((2, 8, 16, 512), BF16),
            vmem((2, 8, 16, 512), BF16),
            vmem((8, 16, UNITS), F32),
            vmem((64, UNITS), F32),
            vmem((NZ, 16, 384), BF16),
            vmem((NZ, 16, 384), BF16),
            vmem((4, 256, D), BF16),
            vmem((4, ROWS, D), BF16),
            vmem((LATENT, 256, D), BF16),
            vmem((D, D), BF16),
            vmem((LATENT, 4, 64, 128), F32),
            dma((7,)),
            dma((NZ,)), dma((NZ,)),
            dma((4, 4)), dma((4, 4)),
            dma((2, NY)), dma((2, NY)),
            dma((NX,)), dma((NX,)),
            dma((4,)), dma((4,)),
            dma((2, 8)), dma((2, 8)),
            dma((NZ,)), dma((NZ,)),
        ],
        compiler_params=pltpu.CompilerParams(
            collective_id=0, has_side_effects=True, vmem_limit_bytes=VMEM_LIMIT
        ),
        cost_estimate=pl.CostEstimate(flops=3 * 10**9, bytes_accessed=10**6, transcendentals=10**5),
        name="encode_patches",
    )(*operands)


def on_device(fields, slot_level, embed_weight, level_encoding, latent_queries, qkv_weight, out_weight):
    out = encode_patches(
        fields, slot_level, latent_queries, qkv_weight, out_weight, embed_weight, level_encoding
    )
    return out.reshape(LATENT, 1, 64, D)


def solution(mesh):
    in_specs = (
        P("lev", "lon", "lat"),
        P("lev"),
        P(),
        P(),
        P(),
        P(None, ("lon", "lev"), None),
        P(("lon", "lev"), None),
    )
    out_specs = P(None, ("lat", "lon", "lev"), None, None)
    return jax.shard_map(
        on_device, mesh=mesh, in_specs=in_specs, out_specs=out_specs, check_vma=False
    )
```

```python
import math

import jax
import jax.numpy as jnp
from jax import lax
from jax.experimental import pallas as pl
from jax.experimental.pallas import tpu as pltpu
from jax.sharding import PartitionSpec as P

MESH = pl.DeviceIdType.MESH
F32 = jnp.float32
BF16 = jnp.bfloat16
NZ, NY, NX, NC = 16, 4, 4, 2
IN = 80
D = 512
LEVELS = 14
HEADS = 16
LATENT = 3
UNITS = 8 * IN
ROWS = LEVELS * 16
VMEM_LIMIT = 40 * 1024 * 1024


def iota(shape, dim):
    return lax.broadcasted_iota(jnp.int32, shape, dim)


def one_hot(mask):
    return jnp.where(mask, 1.0, 0.0).astype(BF16)


def dot(a, b):
    return jnp.dot(a, b, preferred_element_type=F32)


def nt(a, b):
    return lax.dot_general(a, b, (((1,), (1,)), ((), ())), preferred_element_type=F32)


def offset(k):
    return (NZ + (k % 2) * ((k + 1) // 2) - (1 - k % 2) * (k // 2)) % NZ


def loop(lo, hi, act):
    def body(t, carry):
        act(t)
        return carry

    lax.fori_loop(lo, hi, body, 0)


def kernel(
    fields_h, slot_h, latent_h, qkv_h, out_w_h, embed_h, encode_h,
    out,
    fields, slot_level, latent, qkv, out_w, embed, encode,
    tile, wz, pack, w_kv, w_o, q_all, f0, fy, whole, kept, fs, fz,
    shifted, emb, spread, natural_t, mixed,
    in_s, wz_s, wz_r, wp_s, wp_r, wy_s, wy_r, wx_s, wx_r, wc_s, wc_r, fy_s, fy_r, fz_s, fz_r,
):
    x = lax.axis_index("lat")
    lon = lax.axis_index("lon")
    y = lax.axis_index("lev")
    z = lon // 2
    c = lon % 2

    def device(dx=0, dy=0, dz=0, dc=0):
        return {
            "lat": (x + dx) % NX,
            "lon": ((z + dz) % NZ) * 2 + (c + dc) % 2,
            "lev": (y + dy) % NY,
        }

    barrier = pltpu.get_barrier_semaphore()

    def greet(dev):
        pl.semaphore_signal(barrier, inc=1, device_id=dev, device_id_type=MESH)

    loop(1, NZ, lambda k: greet(device(dz=offset(NZ - k))))
    loop(1, NX, lambda t: greet(device(dx=t)))
    loop(1, 8, lambda t: greet(device(dy=t // 2, dc=t % 2)))

    loads = [
        pltpu.make_async_copy(src, dst, in_s.at[i])
        for i, (src, dst) in enumerate(
            (
                (qkv_h, qkv), (out_w_h, out_w), (latent_h, latent), (slot_h, slot_level),
                (fields_h, fields), (embed_h, embed), (encode_h, encode),
            )
        )
    ]
    for load in loads:
        load.start()
    for load in loads[:3]:
        load.wait()

    wq = qkv[0].astype(F32)
    lat = latent[...].astype(F32)
    lane = iota((4, 128), 1)
    q = jnp.zeros((4, 128), F32)
    for a in range(LATENT):
        col = jnp.sum(wq * lat[a : a + 1, :], axis=1, keepdims=True)
        q = jnp.where(lane == a, col, q)
    for part in range(NX):
        cut_at = slice(part * 128, part * 128 + 128)
        tile[part] = jnp.concatenate(
            [q, qkv[1, :, cut_at].astype(F32), qkv[2, :, cut_at].astype(F32), out_w[:, cut_at].astype(F32)],
            axis=0,
        ).astype(BF16)
    wz[0] = tile[x]

    for load in loads[3:5]:
        load.wait()
    at_row = iota((4, 128), 0)
    slot_of_lane = iota((4, 128), 1) // 2
    levels = jnp.full((4, 128), -1.0, F32)
    for s in range(6):
        levels = jnp.where(slot_of_lane == s, slot_level[s].astype(F32), levels)
    for half in (1, 0):
        blocks = []
        for e in range(8):
            to = (z + NZ - offset(8 * half + e)) % NZ
            at = pl.ds(pl.multiple_of(to * UNITS, 128), UNITS)
            blocks.append(jnp.concatenate([fields[s, :, at].astype(F32) for s in range(6)], axis=0))
        for d in range(8):
            units = jnp.concatenate([blocks[e][:, d * IN : (d + 1) * IN] for e in range(8)], axis=1)
            last = units[:, 512:]
            spare = jnp.concatenate([last[0:4], last[4:8], last[8:12], levels], axis=1)
            f0[half, d] = jnp.concatenate([units[:, :512], spare], axis=0).astype(BF16)
    for half in range(2):
        fy[half, c * 4 + y] = f0[half, c * 4 + y]

    def remote(src, dst, send, recv, dev):
        return pltpu.make_async_remote_copy(
            src_ref=src, dst_ref=dst, send_sem=send, recv_sem=recv, device_id=dev, device_id_type=MESH
        )

    def wz_copy(k):
        return remote(tile.at[x], wz.at[k], wz_s.at[k], wz_r.at[k], device(dz=NZ - offset(k)))

    def fy_copy(t, half):
        dev = device(dy=t // 2, dc=t % 2)
        d = (dev["lon"] % 2) * 4 + dev["lev"]
        return remote(f0.at[half, d], fy.at[half, c * 4 + y], fy_s.at[half, t], fy_r.at[half, t], dev)

    def fz_copy(k):
        return remote(fs.at[k], fz.at[z], fz_s.at[k], fz_r.at[k], device(dz=NZ - offset(k)))

    lanes = pl.ds(pl.multiple_of(x * 128, 128), 128)

    def near_y(t):
        return remote(
            pack.at[0, pl.ds(0, 2)], w_kv.at[0, :, c, y, :, :, lanes], wp_s.at[0, t], wp_r.at[0, t], device(dy=t)
        )

    def near_x(t):
        ref = w_kv.at[0, :, c, :, :, :, lanes]
        return remote(ref, ref, wp_s.at[1, t], wp_r.at[1, t], device(dx=t))

    def far_x(t):
        return remote(
            pack.at[1, pl.ds(0, 2)], w_kv.at[1, :, c, y, :, :, lanes], wp_s.at[2, t], wp_r.at[2, t], device(dx=t)
        )

    def far_y(t):
        ref = w_kv.at[1, :, c, y]
        return remote(ref, ref, wp_s.at[3, t], wp_r.at[3, t], device(dy=t))

    def wq_copy(t):
        return remote(pack.at[:, 3], q_all.at[:, c, y], wy_s.at[0, t], wy_r.at[0, t], device(dy=t))

    def wy_copy(t):
        return remote(pack.at[:, 2], w_o.at[:, c, y, :, :, lanes], wy_s.at[1, t], wy_r.at[1, t], device(dy=t))

    def wx_copy(t):
        ref = w_o.at[:, c, :, :, :, lanes]
        return remote(ref, ref, wx_s.at[t], wx_r.at[t], device(dx=t))

    def wc_copy(i, side):
        ref = (w_kv.at[0, :, side], w_kv.at[1, :, side], w_o.at[:, side], q_all.at[:, side])[i]
        return remote(ref, ref, wc_s.at[i], wc_r.at[i], device(dc=1))

    def regroup(half):
        for i in range(2):
            rows = [wz[8 * half + 4 * i + j].astype(F32) for j in range(4)]
            for m, at in enumerate((4, 8, 12, 0)):
                block = jnp.concatenate([r[at : at + 4] for r in rows], axis=0).astype(BF16)
                pack[half, m, i] = block
                if m == 3:
                    q_all[half, c, y, i] = block
                elif m == 2:
                    w_o[half, c, y, i, :, lanes] = block
                else:
                    w_kv[half, m, c, y, i, :, lanes] = block

    pl.semaphore_wait(barrier, NZ - 1 + NX - 1 + 7)
    loop(1, NZ, lambda k: wz_copy(NZ - k).start())
    loop(1, 8, lambda t: fy_copy(t, 1).start())
    for load in loads[5:]:
        load.wait()
    shifted[...] = jnp.zeros_like(shifted)
    starts = (0, IN, 2 * IN - 128, 3 * IN - 128)
    for u in range(4):
        shifted[u, starts[u] : starts[u] + IN, :] = embed[...]

    def head_of(g):
        k = ((g >> 8) << 3) | ((g >> 2) & 7)
        return (z + jnp.where((k & 1) == 1, (k + 1) >> 1, NZ - (k >> 1))) & (NZ - 1)

    g = iota((D, 128), 0)
    place = (head_of(g) * 32 + ((g >> 7) & 1) * 16 + ((g >> 5) & 3) * 4 + (g & 3))[:, :1]
    natural_t[...] = one_hot(iota((D, D), 1) == place)
    ki = iota((256, D), 0) & 127
    head = head_of(iota((1, D), 1))
    for a in range(LATENT):
        spread[a] = one_hot(ki == a * HEADS + head)

    def gather_slots(half):
        for d in range(8):
            part = fy[half, d].astype(F32)
            whole[d, :, 0:512] = part
            whole[d, :, 512:] = jnp.concatenate(
                [part[12:16, 0:128], part[12:16, 128:256], part[12:16, 256:384], jnp.zeros((4, 128), F32)], axis=0
            )

    def keep(half, pick):
        kept[...] = dot(pick, whole[...].astype(BF16).reshape(128, UNITS))
        for e in range(8):
            fs[8 * half + e] = jnp.concatenate(
                [kept[16 * u : 16 * u + 16, e * IN : (e + 1) * IN] for u in range(4)] + [blank], axis=1
            ).astype(BF16)

    loop(1, 8, lambda k: wz_copy(k).wait_recv())
    regroup(0)
    loop(1, NY, lambda t: near_y(t).start())
    loop(1, 8, lambda t: fy_copy(t, 1).wait_recv())
    loop(1, 8, lambda t: fy_copy(t, 0).start())
    blank = jnp.zeros((16, 64), F32)
    at_row = iota((16, 128), 0)
    at_lane = iota((16, 128), 1)
    picks = []
    for d in range(8):
        listed = fy[1, d, :, 384:512].astype(F32)[12:13]
        level = jnp.sum(jnp.where(at_row == at_lane, listed, 0.0), axis=1, keepdims=True)
        picks.append(
            jnp.where(
                (level == (at_lane % 16).astype(F32)) & (at_row < 12)
                & (at_lane // 32 == d // 4) & (at_row % 2 == (at_lane // 16) % 2),
                1.0,
                0.0,
            )
        )
    pick = jnp.transpose(jnp.concatenate(picks, axis=0))[:64].astype(BF16)
    gather_slots(1)
    keep(1, pick)
    loop(0, 8, lambda k: fz_copy(NZ - 1 - k).start())
    loop(8, NZ, lambda k: wz_copy(k).wait_recv())
    regroup(1)
    loop(1, NX, lambda t: far_x(t).start())
    loop(1, NY, lambda t: wq_copy(t).start())
    loop(1, NY, lambda t: wy_copy(t).start())
    loop(1, NY, lambda t: near_y(t).wait_recv())
    loop(1, NX, lambda t: near_x(t).start())
    loop(1, 8, lambda t: fy_copy(t, 0).wait_recv())
    gather_slots(0)
    keep(0, pick)
    loop(1, 8, lambda k: fz_copy(8 - k).start())
    fz[z] = fs[0]
    loop(1, NX, lambda t: far_x(t).wait_recv())
    loop(1, NY, lambda t: far_y(t).start())
    loop(1, NY, lambda t: wq_copy(t).wait_recv())
    wc_copy(3, c).start()
    loop(1, NY, lambda t: wy_copy(t).wait_recv())
    loop(1, NX, lambda t: wx_copy(t).start())
    loop(1, NX, lambda t: near_x(t).wait_recv())
    wc_copy(0, c).start()

    loop(1, NY, lambda t: far_y(t).wait_recv())
    wc_copy(1, c).start()
    loop(1, NZ, lambda k: fz_copy(k).wait_recv())
    r = iota((ROWS, 256), 0)
    j = iota((ROWS, 256), 1)
    rows = dot(one_hot(j == (r % 16) * 16 + r // 16), fz[...].reshape(256, 384)).astype(BF16)
    encoding = jnp.broadcast_to(encode[...].astype(F32)[:, None, :], (LEVELS, 16, D)).reshape(ROWS, D)
    for u, (lo, hi) in enumerate(((0, 128), (0, 256), (128, 256), (128, 384))):
        emb[u] = (dot(rows[:, lo:hi], shifted[u, : hi - lo, :]) + encoding).astype(BF16)

    scale = 1.0 / math.sqrt(D // HEADS)

    def attend(half):
        g = iota((256, 128), 0) + 256 * half
        at_lane = iota((256, 128), 1)
        qv = q_all[half].astype(F32).reshape(256, 128)
        found = jnp.zeros((256, 128), F32)
        for a in range(LATENT):
            found = jnp.where(at_lane == a * HEADS + head_of(g), qv[:, a : a + 1], found)
        found = found.astype(BF16)
        k_w = w_kv[half, 0].reshape(256, D)
        v_w = w_kv[half, 1].reshape(256, D)
        cut_at = slice(256 * half, 256 * half + 256)
        rows = emb[...].reshape(4 * ROWS, D)
        keys = nt(rows, k_w).astype(BF16)
        scores = (dot(keys, found) * scale).reshape(4, LEVELS, 16, 128)
        highest = jnp.max(scores, axis=1, keepdims=True)
        expo = jnp.exp(scores - highest)
        weight = (expo * (1.0 / jnp.sum(expo, axis=1, keepdims=True))).reshape(4 * ROWS, 128)
        top = weight.astype(BF16)
        low = (weight - top.astype(F32)).astype(BF16)
        both = jnp.concatenate([top, low], axis=1)
        values = nt(rows, v_w).astype(BF16).astype(F32)
        for a in range(LATENT):
            if a < 2:
                wide = dot(both, spread[a, :, cut_at])
            else:
                wide = jnp.concatenate(
                    [
                        jnp.take_along_axis(
                            weight,
                            head_of(iota((4 * ROWS, 128), 1) + 256 * half + 128 * i) + a * HEADS,
                            axis=1,
                            mode="promise_in_bounds",
                        )
                        for i in range(2)
                    ],
                    axis=1,
                )
            total = jnp.sum((wide * values).reshape(4, LEVELS, 16, 256), axis=1)
            for u in range(4):
                mixed[a, 2 * half, pl.ds(u, 16, 4), :] = total[u, :, :128]
                mixed[a, 2 * half + 1, pl.ds(u, 16, 4), :] = total[u, :, 128:]

    loop(1, NX, lambda t: wx_copy(t).wait_recv())
    wc_copy(2, c).start()
    wc_copy(3, 1 - c).wait_recv()
    wc_copy(0, 1 - c).wait_recv()
    attend(0)
    wc_copy(1, 1 - c).wait_recv()
    attend(1)
    block = jnp.concatenate(
        [jnp.concatenate([mixed[a, i] for i in range(4)], axis=1) for a in range(LATENT)], axis=0
    ).astype(BF16)
    block = dot(block, natural_t[...]).astype(BF16)
    wc_copy(2, 1 - c).wait_recv()
    block = nt(block, w_o[...].reshape(D, D)).astype(BF16)
    out[...] = dot(block, natural_t[...]).astype(BF16).reshape(LATENT, 64, D)

    loop(1, NZ, lambda k: wz_copy(k).wait_send())
    loop(1, NZ, lambda k: fz_copy(k).wait_send())
    for half in range(2):
        loop(1, 8, lambda t: fy_copy(t, half).wait_send())
    loop(1, NY, lambda t: near_y(t).wait_send())
    loop(1, NX, lambda t: near_x(t).wait_send())
    loop(1, NX, lambda t: far_x(t).wait_send())
    loop(1, NY, lambda t: far_y(t).wait_send())
    loop(1, NY, lambda t: wq_copy(t).wait_send())
    loop(1, NY, lambda t: wy_copy(t).wait_send())
    loop(1, NX, lambda t: wx_copy(t).wait_send())
    for i in range(4):
        wc_copy(i, c).wait_send()


def encode_patches(*operands):
    dma = pltpu.SemaphoreType.DMA
    vmem = pltpu.VMEM
    fields, slot_level, latent, qkv, out_w, embed, encode = operands
    operands = [pltpu.with_memory_space_constraint(o, pltpu.HBM) for o in operands]
    return pl.pallas_call(
        kernel,
        out_shape=jax.ShapeDtypeStruct((LATENT, 64, D), BF16),
        in_specs=[pl.BlockSpec(memory_space=pltpu.HBM)] * 7,
        out_specs=pl.BlockSpec(memory_space=pltpu.VMEM),
        scratch_shapes=[
            vmem(fields.shape, BF16),
            pltpu.SMEM(slot_level.shape, jnp.int32),
            vmem(latent.shape, BF16),
            vmem(qkv.shape, BF16),
            vmem(out_w.shape, BF16),
            vmem(embed.shape, BF16),
            vmem(encode.shape, BF16),
            vmem((NX, 16, 128), BF16),
            vmem((NZ, 16, 128), BF16),
            vmem((2, 4, 2, 16, 128), BF16),
            vmem((2, 2, NC, NY, 2, 16, D), BF16),
            vmem((2, NC, NY, 2, 16, D), BF16),
            vmem((2, NC, NY, 2, 16, 128), BF16),
            vmem((2, 8, 16, 512), BF16),
            vmem((2, 8, 16, 512), BF16),
            vmem((8, 16, UNITS), F32),
            vmem((64, UNITS), F32),
            vmem((NZ, 16, 384), BF16),
            vmem((NZ, 16, 384), BF16),
            vmem((4, 256, D), BF16),
            vmem((4, ROWS, D), BF16),
            vmem((LATENT, 256, D), BF16),
            vmem((D, D), BF16),
            vmem((LATENT, 4, 64, 128), F32),
            dma((7,)),
            dma((NZ,)), dma((NZ,)),
            dma((4, 4)), dma((4, 4)),
            dma((2, NY)), dma((2, NY)),
            dma((NX,)), dma((NX,)),
            dma((4,)), dma((4,)),
            dma((2, 8)), dma((2, 8)),
            dma((NZ,)), dma((NZ,)),
        ],
        compiler_params=pltpu.CompilerParams(
            collective_id=0, has_side_effects=True, vmem_limit_bytes=VMEM_LIMIT
        ),
        cost_estimate=pl.CostEstimate(flops=3 * 10**9, bytes_accessed=10**6, transcendentals=10**5),
        name="encode_patches",
    )(*operands)


def on_device(fields, slot_level, embed_weight, level_encoding, latent_queries, qkv_weight, out_weight):
    out = encode_patches(
        fields, slot_level, latent_queries, qkv_weight, out_weight, embed_weight, level_encoding
    )
    return out.reshape(LATENT, 1, 64, D)


def solution(mesh):
    in_specs = (
        P("lev", "lon", "lat"),
        P("lev"),
        P(),
        P(),
        P(),
        P(None, ("lon", "lev"), None),
        P(("lon", "lev"), None),
    )
    out_specs = P(None, ("lat", "lon", "lev"), None, None)
    return jax.shard_map(
        on_device, mesh=mesh, in_specs=in_specs, out_specs=out_specs, check_vma=False
    )
```
